32 devices in a mesh: ctx: 8 (over y, x, core), tp: 4 (over z).
Axes of the slice: x: 2, y: 2, z: 4, core: 2. Of those that a mesh axis runs over, the one named last changes fastest.
Arguments:
- tokens: bfloat16 [768, 4096], P(('ctx', 'tp')), may hold values from -6 to 6
- proj_weight: bfloat16 [4096, 3, 3072], P(None, None, 'tp'), may hold values from -0.09375 to 0.09375
- feat_taps: float32 [3, 3, 3072], P(None, None, 'tp'), may hold values from -2.5 to 2.5
- inner_taps: float32 [7, 3072], P(None, 'tp'), may hold values from -2.5 to 2.5
- grad_out: bfloat16 [768, 3072], P('ctx', 'tp'), may hold values from -6 to 6
Outputs:
- gated: bfloat16 [768, 3072], P('ctx', 'tp')
- grad_tokens: bfloat16 [768, 4096], P(('ctx', 'tp'))
The draws below stay inside these ranges and needn't reach their ends.
All inputs are finite; a program needn't handle non-finite values.
Results may differ from the reference program's by a relative error of at most 0.025.
Values may be sent and summed in bfloat16 or wider, within the bound.
A program may use at most 64 MiB of HBM per device.

```python
import jax
import jax.numpy as jnp
from jax import lax

D = 4096
FTAPS = 3
ITAPS = 7
CH = 3072
SEQ = 768
N_TP = 4


def block_scale(key, shape, cuts, low, top_value):
    gain = 1.0
    for position, shards_of in cuts:
        steps = jax.random.uniform(jax.random.fold_in(jax.random.fold_in(key, 6), position), (shards_of,), jnp.float32, low / len(cuts), top_value / len(cuts))
        gain = gain * jnp.repeat(jnp.exp(steps), shape[position] // shards_of).reshape((-1,) + (1,) * (len(shape) - 1 - position))
    return gain


def noise(stream_key, dims, deviation, reach, pieces=(), dtype=jnp.bfloat16):
    factor_of = block_scale(stream_key, dims, pieces, -0.22, 0.18) if pieces else 1.0
    drawn = jax.random.normal(stream_key, dims, jnp.float32) * deviation * factor_of
    return jnp.minimum(jnp.maximum(drawn, -reach), reach).astype(dtype)


def setup_inputs(seed: int = 0) -> dict:
    keys = jax.random.split(jax.random.key(seed), 6)
    return {
        "tokens": noise(keys[0], (SEQ, D), 1.0, 6.0, ((0, 32),)),
        "proj_weight": noise(keys[1], (D, 3, CH), D ** -0.5, 0.09375, ((2, 4),)),
        "feat_taps": noise(keys[2], (3, FTAPS, CH), 0.6, 2.5, ((2, 4),), jnp.float32),
        "inner_taps": noise(keys[3], (ITAPS, CH), 0.4, 2.5, ((1, 4),), jnp.float32),
        "grad_out": noise(keys[4], (SEQ, CH), 1.0, 6.0, ((0, 8), (1, 4))),
    }


def causal_taps(series, kernel):
    taps = kernel.shape[0]
    length = series.shape[0] - (taps - 1)
    summed = kernel[0] * series[taps - 1:taps - 1 + length]
    for offset in range(1, taps):
        summed = summed + kernel[offset] * series[taps - 1 - offset:taps - 1 - offset + length]
    return summed


def anti_taps(series, kernel):
    taps = kernel.shape[0]
    length = series.shape[0] - (taps - 1)
    summed = kernel[0] * series[0:length]
    for offset in range(1, taps):
        summed = summed + kernel[offset] * series[offset:offset + length]
    return summed


def featurize(window, feat_taps, inner_taps):
    query_feat = causal_taps(window[6:, 0], feat_taps[0])
    key_feat = causal_taps(window[:, 1], feat_taps[1])
    value_feat = causal_taps(window[:, 2], feat_taps[2])
    inner_conv = causal_taps(key_feat * value_feat, inner_taps)
    return query_feat, key_feat, value_feat, inner_conv


def reference(tokens, proj_weight, feat_taps, inner_taps, grad_out):
    flat_weight = proj_weight.reshape(D, 3 * CH)
    projected = jnp.dot(tokens, flat_weight, preferred_element_type=jnp.float32).astype(jnp.bfloat16)
    projected = projected.reshape(SEQ, 3, CH).astype(jnp.float32)
    window = jnp.concatenate([jnp.zeros((8, 3, CH), jnp.float32), projected], axis=0)
    query_feat, key_feat, value_feat, inner_conv = featurize(window, feat_taps, inner_taps)
    gated = (query_feat * inner_conv).astype(jnp.bfloat16)
    grad_f = grad_out.astype(jnp.float32)
    grad_query = grad_f * inner_conv
    grad_inner = grad_f * query_feat
    grad_mix = anti_taps(jnp.concatenate([grad_inner, jnp.zeros((6, CH), jnp.float32)], axis=0), inner_taps)
    grad_key = grad_mix * value_feat[6:]
    grad_value = grad_mix * key_feat[6:]
    pad_two = jnp.zeros((2, CH), jnp.float32)
    grad_proj = jnp.stack([
        anti_taps(jnp.concatenate([grad_query, pad_two], axis=0), feat_taps[0]),
        anti_taps(jnp.concatenate([grad_key, pad_two], axis=0), feat_taps[1]),
        anti_taps(jnp.concatenate([grad_value, pad_two], axis=0), feat_taps[2])], axis=1)
    grad_proj = grad_proj.astype(jnp.bfloat16)
    group = CH // N_TP
    total = jnp.zeros((SEQ, D), jnp.float32)
    for index in range(N_TP):
        part_grad = grad_proj[:, :, index * group:(index + 1) * group].reshape(SEQ, 3 * group)
        part_weight = proj_weight[:, :, index * group:(index + 1) * group].reshape(D, 3 * group)
        partial_sum = lax.dot_general(part_grad, part_weight, (((1,), (1,)), ((), ())), preferred_element_type=jnp.float32)
        total = total + partial_sum.astype(jnp.bfloat16).astype(jnp.float32)
    return gated, total.astype(jnp.bfloat16)
```

```python
import functools

import jax
import jax.numpy as jnp
from jax import lax
from jax.experimental import pallas as pl
from jax.experimental.pallas import tpu as pltpu
from jax.sharding import PartitionSpec as P

MESH = pl.DeviceIdType.MESH
F32 = jnp.float32
BF16 = jnp.bfloat16
PIECES = 4
HALO = 8


def kernel(
    n,
    n_ctx,
    tokens,
    weight_hbm,
    feat_taps,
    inner_taps,
    grad_out,
    gated,
    grad_tokens,
    weight,
    blocks,
    stack,
    ext,
    grads,
    mix,
    dinner,
    dfeat,
    dproj,
    edge,
    halo,
    grad_edge,
    grad_halo,
    partial,
    outgoing,
    from_left,
    from_right,
    weight_sem,
    gather_recv,
    gather_right,
    gather_left,
    scatter_send,
    left_recv,
    right_recv,
    halo_send,
    halo_recv,
):
    z = lax.axis_index("tp")
    ctx = lax.axis_index("ctx")
    rows, width = tokens.shape
    total, channels = gated.shape
    cut = width // PIECES

    def weight_copy(piece, part):
        span = pl.ds(piece * cut, cut)
        return pltpu.make_async_copy(
            weight_hbm.at[part, span, :], weight.at[part, span, :], weight_sem.at[piece, part]
        )

    for piece in range(PIECES):
        for part in range(3):
            weight_copy(piece, part).start()

    has_left, has_right = z > 0, z < n - 1
    has_before, has_after = ctx > 0, ctx < n_ctx - 1
    barrier = pltpu.get_barrier_semaphore()

    def greet(here, axis, index):
        @pl.when(here)
        def _():
            pl.semaphore_signal(barrier, inc=1, device_id={axis: index}, device_id_type=MESH)

    greet(has_left, "tp", z - 1)
    greet(has_right, "tp", z + 1)
    greet(has_before, "ctx", ctx - 1)
    greet(has_after, "ctx", ctx + 1)

    for piece in range(PIECES):
        blocks[piece, z] = tokens[:, piece * cut : (piece + 1) * cut]
    grads[0:total, :] = grad_out[...].astype(F32)
    grad_edge[...] = grads[0:HALO, :]

    peers = sum(
        here.astype(jnp.int32) for here in (has_left, has_right, has_before, has_after)
    )
    pl.semaphore_wait(barrier, peers)

    def to_right(piece, block):
        return pltpu.make_async_remote_copy(
            src_ref=blocks.at[piece, block],
            dst_ref=blocks.at[piece, block],
            send_sem=gather_right.at[piece, block],
            recv_sem=gather_recv.at[piece, block],
            device_id={"tp": z + 1},
            device_id_type=MESH,
        )

    def to_left(piece, block):
        return pltpu.make_async_remote_copy(
            src_ref=blocks.at[piece, block],
            dst_ref=blocks.at[piece, block],
            send_sem=gather_left.at[piece, block],
            recv_sem=gather_recv.at[piece, block],
            device_id={"tp": z - 1},
            device_id_type=MESH,
        )

    for piece in range(PIECES):

        @pl.when(has_right)
        def _():
            to_right(piece, z).start()

        @pl.when(has_left)
        def _():
            to_left(piece, z).start()

    grad_copy = pltpu.make_async_remote_copy(
        src_ref=grad_edge,
        dst_ref=grad_halo,
        send_sem=halo_send.at[0],
        recv_sem=halo_recv.at[0],
        device_id={"ctx": ctx - 1},
        device_id_type=MESH,
    )

    @pl.when(has_before)
    def _():
        grad_copy.start()

    def gather_step(step, carry):
        for piece in range(PIECES):

            @pl.when(z - step >= 0)
            def _():
                to_right(piece, z - step).wait_recv()

                @pl.when(has_right)
                def _():
                    to_right(piece, z - step).start()

            @pl.when(z + step <= n - 1)
            def _():
                to_left(piece, z + step).wait_recv()

                @pl.when(has_left)
                def _():
                    to_left(piece, z + step).start()

        return carry

    lax.fori_loop(1, n - 1, gather_step, 0)

    for piece in range(PIECES):

        @pl.when(z == n - 1)
        def _():
            to_right(piece, 0).wait_recv()

        @pl.when(z == 0)
        def _():
            to_left(piece, n - 1).wait_recv()

        for block in range(n):
            stack[block * rows : (block + 1) * rows, :] = blocks[piece, block].astype(F32)
        left_side = stack[...].astype(BF16)
        for part in range(3):
            weight_copy(piece, part).wait()
            product = jnp.dot(
                left_side,
                weight[part, piece * cut : (piece + 1) * cut, :],
                preferred_element_type=F32,
            )
            if piece == 0:
                ext[part, HALO : HALO + total, :] = product
            else:
                ext[part, HALO : HALO + total, :] += product

    edge[0] = ext[:, HALO : 2 * HALO, :]
    edge[1] = ext[:, total : total + HALO, :]

    def edge_copy(side, target):
        return pltpu.make_async_remote_copy(
            src_ref=edge.at[side],
            dst_ref=halo.at[side],
            send_sem=halo_send.at[1 + side],
            recv_sem=halo_recv.at[1 + side],
            device_id={"ctx": target},
            device_id_type=MESH,
        )

    first_rows = edge_copy(0, ctx - 1)
    last_rows = edge_copy(1, ctx + 1)

    @pl.when(has_before)
    def _():
        first_rows.start()

    @pl.when(has_after)
    def _():
        last_rows.start()

    @pl.when(has_after)
    def _():
        grad_copy.wait_recv()
        grads[total : total + HALO, :] = grad_halo[...]
        first_rows.wait_recv()
        ext[:, HALO + total :, :] = halo[0]

    @pl.when(ctx == n_ctx - 1)
    def _():
        grads[total : total + HALO, :] = jnp.zeros((HALO, channels), F32)
        ext[:, HALO + total :, :] = jnp.zeros((3, HALO, channels), F32)

    @pl.when(has_before)
    def _():
        last_rows.wait_recv()
        ext[:, 0:HALO, :] = halo[1]

    @pl.when(ctx == 0)
    def _():
        ext[:, 0:HALO, :] = jnp.zeros((3, HALO, channels), F32)

    long = total + HALO
    lanes = 128

    def channel_step(index, carry):
        at = pl.ds(pl.multiple_of(index * lanes, lanes), lanes)

        def conv(part, start):
            terms = feat_taps[part, 0:1, at] * ext[part, start : start + long, at]
            for tap in range(1, 3):
                terms += (
                    feat_taps[part, tap : tap + 1, at]
                    * ext[part, start - tap : start - tap + long, at]
                )
            return terms

        query = conv(0, HALO)
        dinner[0:long, :] = grads[:, at] * query
        key = conv(1, 2)
        value = conv(2, 2)
        mix[0:long, :] = key * value
        dfeat[1, 0:long, :] = value
        dfeat[2, 0:long, :] = key
        inner = inner_taps[0:1, at] * mix[6 : 6 + long, :]
        for tap in range(1, 7):
            inner += inner_taps[tap : tap + 1, at] * mix[6 - tap : 6 - tap + long, :]
        gated[:, at] = (query * inner)[0:total].astype(BF16)
        dfeat[0, 0:long, :] = grads[:, at] * inner
        dmix = inner_taps[0:1, at] * dinner[0:long, :]
        for tap in range(1, 7):
            dmix += inner_taps[tap : tap + 1, at] * dinner[tap : tap + long, :]
        dkey = dmix * dfeat[1, 6 : 6 + long, :]
        dvalue = dmix * dfeat[2, 6 : 6 + long, :]
        dfeat[1, 0:long, :] = dkey
        dfeat[2, 0:long, :] = dvalue
        for part in range(3):
            series = feat_taps[part, 0:1, at] * dfeat[part, 0:total, :]
            for tap in range(1, 3):
                series += feat_taps[part, tap : tap + 1, at] * dfeat[part, tap : tap + total, :]
            dproj[part, :, at] = series.astype(BF16)
        return carry

    tail = jnp.zeros((HALO, lanes), F32)
    mix[long:, :] = tail
    dinner[long:, :] = tail
    for part in range(3):
        dfeat[part, long:, :] = tail
    lax.fori_loop(0, channels // lanes, channel_step, 0)

    def pass_right(piece, block):
        return pltpu.make_async_remote_copy(
            src_ref=outgoing.at[piece, block],
            dst_ref=from_left.at[piece, block],
            send_sem=scatter_send.at[piece, block],
            recv_sem=left_recv.at[piece, block],
            device_id={"tp": z + 1},
            device_id_type=MESH,
        )

    def pass_left(piece, block):
        return pltpu.make_async_remote_copy(
            src_ref=outgoing.at[piece, block],
            dst_ref=from_right.at[piece, block],
            send_sem=scatter_send.at[piece, block],
            recv_sem=right_recv.at[piece, block],
            device_id={"tp": z - 1},
            device_id_type=MESH,
        )

    def begin(piece):
        def step_of(step, carry):
            far, near = n - 1 - step, step

            @pl.when(z == 0)
            def _():
                outgoing[piece, far] = partial[piece, far].astype(BF16)
                pass_right(piece, far).start()

            @pl.when(z == n - 1)
            def _():
                outgoing[piece, near] = partial[piece, near].astype(BF16)
                pass_left(piece, near).start()

            return carry

        lax.fori_loop(0, n - 1, step_of, 0)

    def forward(piece):
        def step_of(step, carry):
            far, near = n - 1 - step, step

            @pl.when((z > 0) & (z < far))
            def _():
                pass_right(piece, far).wait_recv()
                outgoing[piece, far] = (
                    from_left[piece, far].astype(F32) + partial[piece, far]
                ).astype(BF16)
                pass_right(piece, far).start()

            @pl.when((z < n - 1) & (z > near))
            def _():
                pass_left(piece, near).wait_recv()
                outgoing[piece, near] = (
                    from_right[piece, near].astype(F32) + partial[piece, near]
                ).astype(BF16)
                pass_left(piece, near).start()

            return carry

        lax.fori_loop(0, n - 1, step_of, 0)

    for piece in range(PIECES):
        share = jnp.zeros((total, cut), F32)
        for part in range(3):
            share += lax.dot_general(
                dproj[part],
                weight[part, piece * cut : (piece + 1) * cut, :],
                (((1,), (1,)), ((), ())),
                preferred_element_type=F32,
            )
        for block in range(n):
            partial[piece, block] = share[block * rows : (block + 1) * rows]
        begin(piece)
        if piece > 0:
            forward(piece - 1)
    forward(PIECES - 1)

    for piece in range(PIECES):

        @pl.when(has_left)
        def _():
            pass_right(piece, z).wait_recv()
            partial[piece, z] += from_left[piece, z].astype(F32)

        @pl.when(has_right)
        def _():
            pass_left(piece, z).wait_recv()
            partial[piece, z] += from_right[piece, z].astype(F32)

        grad_tokens[:, piece * cut : (piece + 1) * cut] = partial[piece, z].astype(BF16)

    @pl.when(has_before)
    def _():
        grad_copy.wait_send()
        first_rows.wait_send()

    @pl.when(has_after)
    def _():
        last_rows.wait_send()

    def drain(block, carry):
        for piece in range(PIECES):

            @pl.when(has_right & (block <= z))
            def _():
                to_right(piece, block).wait_send()

            @pl.when(has_left & (block >= z))
            def _():
                to_left(piece, block).wait_send()

            @pl.when(block != z)
            def _():
                pass_right(piece, block).wait_send()

        return carry

    lax.fori_loop(0, n, drain, 0)


def local(n, n_ctx, tokens, proj_weight, feat_taps, inner_taps, grad_out):
    rows, width = tokens.shape
    total, channels = grad_out.shape
    cut = width // PIECES
    weight = jnp.transpose(proj_weight, (1, 0, 2))
    vmem = pl.BlockSpec(memory_space=pltpu.VMEM)
    dma = pltpu.SemaphoreType.DMA
    long = total + 2 * HALO
    return pl.pallas_call(
        functools.partial(kernel, n, n_ctx),
        out_shape=(
            jax.ShapeDtypeStruct((total, channels), BF16),
            jax.ShapeDtypeStruct((rows, width), BF16),
        ),
        in_specs=[vmem, pl.BlockSpec(memory_space=pl.ANY), vmem, vmem, vmem],
        out_specs=(vmem, vmem),
        scratch_shapes=[
            pltpu.VMEM((3, width, channels), BF16),
            pltpu.VMEM((PIECES, n, rows, cut), BF16),
            pltpu.VMEM((total, cut), F32),
            pltpu.VMEM((3, long, channels), F32),
            pltpu.VMEM((total + HALO, channels), F32),
            pltpu.VMEM((long, 128), F32),
            pltpu.VMEM((long, 128), F32),
            pltpu.VMEM((3, long, 128), F32),
            pltpu.VMEM((3, total, channels), BF16),
            pltpu.VMEM((2, 3, HALO, channels), F32),
            pltpu.VMEM((2, 3, HALO, channels), F32),
            pltpu.VMEM((HALO, channels), F32),
            pltpu.VMEM((HALO, channels), F32),
            pltpu.VMEM((PIECES, n, rows, cut), F32),
            pltpu.VMEM((PIECES, n, rows, cut), BF16),
            pltpu.VMEM((PIECES, n, rows, cut), BF16),
            pltpu.VMEM((PIECES, n, rows, cut), BF16),
            dma((PIECES, 3)),
            dma((PIECES, n)),
            dma((PIECES, n)),
            dma((PIECES, n)),
            dma((PIECES, n)),
            dma((PIECES, n)),
            dma((PIECES, n)),
            dma((3,)),
            dma((3,)),
        ],
        compiler_params=pltpu.CompilerParams(
            collective_id=0, has_side_effects=True, vmem_limit_bytes=50 * 1024 * 1024
        ),
        cost_estimate=pl.CostEstimate(
            flops=4 * total * width * 3 * channels,
            bytes_accessed=6 * width * channels,
            transcendentals=0,
        ),
    )(tokens, weight, feat_taps, inner_taps, grad_out)


def solution(mesh):
    in_specs = (
        P(("ctx", "tp"), None),
        P(None, None, "tp"),
        P(None, None, "tp"),
        P(None, "tp"),
        P("ctx", "tp"),
    )
    out_specs = (P("ctx", "tp"), P(("ctx", "tp"), None))
    body = functools.partial(local, mesh.shape["tp"], mesh.shape["ctx"])
    return jax.shard_map(
        body, mesh=mesh, in_specs=in_specs, out_specs=out_specs, check_vma=False
    )
```

```python
import functools

import jax
import jax.numpy as jnp
from jax import lax
from jax.experimental import pallas as pl
from jax.experimental.pallas import tpu as pltpu
from jax.sharding import PartitionSpec as P

MESH = pl.DeviceIdType.MESH
F32 = jnp.float32
BF16 = jnp.bfloat16
PIECES = 4
HALO = 8


def kernel(
    n,
    n_ctx,
    tokens,
    weight_hbm,
    feat_hbm,
    inner_hbm,
    grad_hbm,
    gated,
    grad_tokens,
    feat_taps,
    inner_taps,
    grad_out,
    weight,
    blocks,
    stack,
    ext,
    grads,
    mix,
    dinner,
    dfeat,
    dproj,
    edge,
    halo,
    grad_edge,
    grad_halo,
    partial,
    outgoing,
    from_left,
    from_right,
    weight_sem,
    gather_recv,
    gather_right,
    gather_left,
    scatter_send,
    left_recv,
    right_recv,
    halo_send,
    halo_recv,
    token_sem,
    small_sem,
):
    z = lax.axis_index("tp")
    ctx = lax.axis_index("ctx")
    rows, width = tokens.shape
    total, channels = gated.shape
    cut = width // PIECES

    def weight_copy(piece, part):
        span = pl.ds(piece * cut, cut)
        return pltpu.make_async_copy(
            weight_hbm.at[part, span, :], weight.at[part, span, :], weight_sem.at[piece, part]
        )

    own = [
        pltpu.make_async_copy(
            tokens.at[:, pl.ds(piece * cut, cut)], blocks.at[piece, z], token_sem.at[piece]
        )
        for piece in range(PIECES)
    ]
    small = [
        pltpu.make_async_copy(source, target, small_sem.at[index])
        for index, (source, target) in enumerate(
            ((grad_hbm, grad_out), (feat_hbm, feat_taps), (inner_hbm, inner_taps))
        )
    ]
    for copy in own + small:
        copy.start()
    for piece in range(PIECES):
        for part in range(3):
            weight_copy(piece, part).start()

    has_left, has_right = z > 0, z < n - 1
    has_before, has_after = ctx > 0, ctx < n_ctx - 1
    barrier = pltpu.get_barrier_semaphore()

    def greet(here, axis, index):
        @pl.when(here)
        def _():
            pl.semaphore_signal(barrier, inc=1, device_id={axis: index}, device_id_type=MESH)

    greet(has_left, "tp", z - 1)
    greet(has_right, "tp", z + 1)
    greet(has_before, "ctx", ctx - 1)
    greet(has_after, "ctx", ctx + 1)

    for copy in own + small:
        copy.wait()
    grads[0:total, :] = grad_out[...].astype(F32)
    grad_edge[...] = grads[0:HALO, :]

    peers = sum(
        here.astype(jnp.int32) for here in (has_left, has_right, has_before, has_after)
    )
    pl.semaphore_wait(barrier, peers)

    def to_right(piece, block):
        return pltpu.make_async_remote_copy(
            src_ref=blocks.at[piece, block],
            dst_ref=blocks.at[piece, block],
            send_sem=gather_right.at[piece, block],
            recv_sem=gather_recv.at[piece, block],
            device_id={"tp": z + 1},
            device_id_type=MESH,
        )

    def to_left(piece, block):
        return pltpu.make_async_remote_copy(
            src_ref=blocks.at[piece, block],
            dst_ref=blocks.at[piece, block],
            send_sem=gather_left.at[piece, block],
            recv_sem=gather_recv.at[piece, block],
            device_id={"tp": z - 1},
            device_id_type=MESH,
        )

    for piece in range(PIECES):

        @pl.when(has_right)
        def _():
            to_right(piece, z).start()

        @pl.when(has_left)
        def _():
            to_left(piece, z).start()

    grad_copy = pltpu.make_async_remote_copy(
        src_ref=grad_edge,
        dst_ref=grad_halo,
        send_sem=halo_send.at[0],
        recv_sem=halo_recv.at[0],
        device_id={"ctx": ctx - 1},
        device_id_type=MESH,
    )

    @pl.when(has_before)
    def _():
        grad_copy.start()

    def gather_step(step, carry):
        for piece in range(PIECES):

            @pl.when(z - step >= 0)
            def _():
                to_right(piece, z - step).wait_recv()

                @pl.when(has_right)
                def _():
                    to_right(piece, z - step).start()

            @pl.when(z + step <= n - 1)
            def _():
                to_left(piece, z + step).wait_recv()

                @pl.when(has_left)
                def _():
                    to_left(piece, z + step).start()

        return carry

    lax.fori_loop(1, n - 1, gather_step, 0)

    for piece in range(PIECES):

        @pl.when(z == n - 1)
        def _():
            to_right(piece, 0).wait_recv()

        @pl.when(z == 0)
        def _():
            to_left(piece, n - 1).wait_recv()

        for block in range(n):
            stack[block * rows : (block + 1) * rows, :] = blocks[piece, block].astype(F32)
        left_side = stack[...].astype(BF16)
        for part in range(3):
            weight_copy(piece, part).wait()
            product = jnp.dot(
                left_side,
                weight[part, piece * cut : (piece + 1) * cut, :],
                preferred_element_type=F32,
            )
            if piece == 0:
                ext[part, HALO : HALO + total, :] = product
            else:
                ext[part, HALO : HALO + total, :] += product

    edge[0] = ext[:, HALO : 2 * HALO, :]
    edge[1] = ext[:, total : total + HALO, :]

    def edge_copy(side, target):
        return pltpu.make_async_remote_copy(
            src_ref=edge.at[side],
            dst_ref=halo.at[side],
            send_sem=halo_send.at[1 + side],
            recv_sem=halo_recv.at[1 + side],
            device_id={"ctx": target},
            device_id_type=MESH,
        )

    first_rows = edge_copy(0, ctx - 1)
    last_rows = edge_copy(1, ctx + 1)

    @pl.when(has_before)
    def _():
        first_rows.start()

    @pl.when(has_after)
    def _():
        last_rows.start()

    @pl.when(has_after)
    def _():
        grad_copy.wait_recv()
        grads[total : total + HALO, :] = grad_halo[...]
        first_rows.wait_recv()
        ext[:, HALO + total :, :] = halo[0]

    @pl.when(ctx == n_ctx - 1)
    def _():
        grads[total : total + HALO, :] = jnp.zeros((HALO, channels), F32)
        ext[:, HALO + total :, :] = jnp.zeros((3, HALO, channels), F32)

    @pl.when(has_before)
    def _():
        last_rows.wait_recv()
        ext[:, 0:HALO, :] = halo[1]

    @pl.when(ctx == 0)
    def _():
        ext[:, 0:HALO, :] = jnp.zeros((3, HALO, channels), F32)

    long = total + HALO
    lanes = 128

    def channel_step(index, carry):
        at = pl.ds(pl.multiple_of(index * lanes, lanes), lanes)

        def conv(part, start):
            terms = feat_taps[part, 0:1, at] * ext[part, start : start + long, at]
            for tap in range(1, 3):
                terms += (
                    feat_taps[part, tap : tap + 1, at]
                    * ext[part, start - tap : start - tap + long, at]
                )
            return terms

        query = conv(0, HALO)
        dinner[0:long, :] = grads[:, at] * query
        key = conv(1, 2)
        value = conv(2, 2)
        mix[0:long, :] = key * value
        dfeat[1, 0:long, :] = value
        dfeat[2, 0:long, :] = key
        inner = inner_taps[0:1, at] * mix[6 : 6 + long, :]
        for tap in range(1, 7):
            inner += inner_taps[tap : tap + 1, at] * mix[6 - tap : 6 - tap + long, :]
        gated[:, at] = (query * inner)[0:total].astype(BF16)
        dfeat[0, 0:long, :] = grads[:, at] * inner
        dmix = inner_taps[0:1, at] * dinner[0:long, :]
        for tap in range(1, 7):
            dmix += inner_taps[tap : tap + 1, at] * dinner[tap : tap + long, :]
        dkey = dmix * dfeat[1, 6 : 6 + long, :]
        dvalue = dmix * dfeat[2, 6 : 6 + long, :]
        dfeat[1, 0:long, :] = dkey
        dfeat[2, 0:long, :] = dvalue
        for part in range(3):
            series = feat_taps[part, 0:1, at] * dfeat[part, 0:total, :]
            for tap in range(1, 3):
                series += feat_taps[part, tap : tap + 1, at] * dfeat[part, tap : tap + total, :]
            dproj[part, :, at] = series.astype(BF16)
        return carry

    tail = jnp.zeros((HALO, lanes), F32)
    mix[long:, :] = tail
    dinner[long:, :] = tail
    for part in range(3):
        dfeat[part, long:, :] = tail
    lax.fori_loop(0, channels // lanes, channel_step, 0)

    def pass_right(piece, block):
        return pltpu.make_async_remote_copy(
            src_ref=outgoing.at[piece, block],
            dst_ref=from_left.at[piece, block],
            send_sem=scatter_send.at[piece, block],
            recv_sem=left_recv.at[piece, block],
            device_id={"tp": z + 1},
            device_id_type=MESH,
        )

    def pass_left(piece, block):
        return pltpu.make_async_remote_copy(
            src_ref=outgoing.at[piece, block],
            dst_ref=from_right.at[piece, block],
            send_sem=scatter_send.at[piece, block],
            recv_sem=right_recv.at[piece, block],
            device_id={"tp": z - 1},
            device_id_type=MESH,
        )

    def begin(piece):
        def step_of(step, carry):
            far, near = n - 1 - step, step

            @pl.when(z == 0)
            def _():
                outgoing[piece, far] = partial[piece, far].astype(BF16)
                pass_right(piece, far).start()

            @pl.when(z == n - 1)
            def _():
                outgoing[piece, near] = partial[piece, near].astype(BF16)
                pass_left(piece, near).start()

            return carry

        lax.fori_loop(0, n - 1, step_of, 0)

    def forward(piece):
        def step_of(step, carry):
            far, near = n - 1 - step, step

            @pl.when((z > 0) & (z < far))
            def _():
                pass_right(piece, far).wait_recv()
                outgoing[piece, far] = (
                    from_left[piece, far].astype(F32) + partial[piece, far]
                ).astype(BF16)
                pass_right(piece, far).start()

            @pl.when((z < n - 1) & (z > near))
            def _():
                pass_left(piece, near).wait_recv()
                outgoing[piece, near] = (
                    from_right[piece, near].astype(F32) + partial[piece, near]
                ).astype(BF16)
                pass_left(piece, near).start()

            return carry

        lax.fori_loop(0, n - 1, step_of, 0)

    for piece in range(PIECES):
        turned = jnp.zeros((cut, total), F32)
        for part in range(3):
            turned += lax.dot_general(
                weight[part, piece * cut : (piece + 1) * cut, :],
                dproj[part],
                (((1,), (1,)), ((), ())),
                preferred_element_type=F32,
            )
        share = turned.T
        for block in range(n):
            partial[piece, block] = share[block * rows : (block + 1) * rows]
        begin(piece)
        if piece > 0:
            forward(piece - 1)
    forward(PIECES - 1)

    for piece in range(PIECES):

        @pl.when(has_left)
        def _():
            pass_right(piece, z).wait_recv()
            partial[piece, z] += from_left[piece, z].astype(F32)

        @pl.when(has_right)
        def _():
            pass_left(piece, z).wait_recv()
            partial[piece, z] += from_right[piece, z].astype(F32)

        grad_tokens[:, piece * cut : (piece + 1) * cut] = partial[piece, z].astype(BF16)

    @pl.when(has_before)
    def _():
        grad_copy.wait_send()
        first_rows.wait_send()

    @pl.when(has_after)
    def _():
        last_rows.wait_send()

    def drain(block, carry):
        for piece in range(PIECES):

            @pl.when(has_right & (block <= z))
            def _():
                to_right(piece, block).wait_send()

            @pl.when(has_left & (block >= z))
            def _():
                to_left(piece, block).wait_send()

            @pl.when(block != z)
            def _():
                pass_right(piece, block).wait_send()

        return carry

    lax.fori_loop(0, n, drain, 0)


def local(n, n_ctx, tokens, proj_weight, feat_taps, inner_taps, grad_out):
    rows, width = tokens.shape
    total, channels = grad_out.shape
    cut = width // PIECES
    weight = jnp.transpose(proj_weight, (1, 0, 2))
    vmem = pl.BlockSpec(memory_space=pltpu.VMEM)
    dma = pltpu.SemaphoreType.DMA
    long = total + 2 * HALO
    return pl.pallas_call(
        functools.partial(kernel, n, n_ctx),
        out_shape=(
            jax.ShapeDtypeStruct((total, channels), BF16),
            jax.ShapeDtypeStruct((rows, width), BF16),
        ),
        in_specs=[pl.BlockSpec(memory_space=pl.ANY)] * 5,
        out_specs=(vmem, vmem),
        scratch_shapes=[
            pltpu.VMEM(feat_taps.shape, F32),
            pltpu.VMEM(inner_taps.shape, F32),
            pltpu.VMEM((total, channels), BF16),
            pltpu.VMEM((3, width, channels), BF16),
            pltpu.VMEM((PIECES, n, rows, cut), BF16),
            pltpu.VMEM((total, cut), F32),
            pltpu.VMEM((3, long, channels), F32),
            pltpu.VMEM((total + HALO, channels), F32),
            pltpu.VMEM((long, 128), F32),
            pltpu.VMEM((long, 128), F32),
            pltpu.VMEM((3, long, 128), F32),
            pltpu.VMEM((3, total, channels), BF16),
            pltpu.VMEM((2, 3, HALO, channels), F32),
            pltpu.VMEM((2, 3, HALO, channels), F32),
            pltpu.VMEM((HALO, channels), F32),
            pltpu.VMEM((HALO, channels), F32),
            pltpu.VMEM((PIECES, n, rows, cut), F32),
            pltpu.VMEM((PIECES, n, rows, cut), BF16),
            pltpu.VMEM((PIECES, n, rows, cut), BF16),
            pltpu.VMEM((PIECES, n, rows, cut), BF16),
            dma((PIECES, 3)),
            dma((PIECES, n)),
            dma((PIECES, n)),
            dma((PIECES, n)),
            dma((PIECES, n)),
            dma((PIECES, n)),
            dma((PIECES, n)),
            dma((3,)),
            dma((3,)),
            dma((PIECES,)),
            dma((3,)),
        ],
        compiler_params=pltpu.CompilerParams(
            collective_id=0, has_side_effects=True, vmem_limit_bytes=58 * 1024 * 1024
        ),
        cost_estimate=pl.CostEstimate(
            flops=4 * total * width * 3 * channels,
            bytes_accessed=6 * width * channels,
            transcendentals=0,
        ),
    )(tokens, weight, feat_taps, inner_taps, grad_out)


def solution(mesh):
    in_specs = (
        P(("ctx", "tp"), None),
        P(None, None, "tp"),
        P(None, None, "tp"),
        P(None, "tp"),
        P("ctx", "tp"),
    )
    out_specs = (P("ctx", "tp"), P(("ctx", "tp"), None))
    body = functools.partial(local, mesh.shape["tp"], mesh.shape["ctx"])
    return jax.shard_map(
        body, mesh=mesh, in_specs=in_specs, out_specs=out_specs, check_vma=False
    )
```

```python
import functools

import jax
import jax.numpy as jnp
from jax import lax
from jax.experimental import pallas as pl
from jax.experimental.pallas import tpu as pltpu
from jax.sharding import PartitionSpec as P

MESH = pl.DeviceIdType.MESH
F32 = jnp.float32
BF16 = jnp.bfloat16
PIECES = 8
HALO = 8


def kernel(
    n,
    n_ctx,
    tokens,
    weight_hbm,
    feat_hbm,
    inner_hbm,
    grad_hbm,
    gated,
    grad_tokens,
    feat_taps,
    inner_taps,
    grad_out,
    weight,
    blocks,
    stack,
    ext,
    grads,
    mix,
    dinner,
    dfeat,
    dproj,
    edge,
    halo,
    grad_edge,
    grad_halo,
    outgoing,
    incoming,
    weight_sem,
    gather_recv,
    gather_send,
    scatter_recv,
    scatter_send,
    halo_send,
    halo_recv,
    token_sem,
    small_sem,
):
    z = lax.axis_index("tp")
    ctx = lax.axis_index("ctx")
    rows, width = tokens.shape
    total, channels = gated.shape
    cut = width // PIECES

    def weight_copy(piece, part):
        span = pl.ds(piece * cut, cut)
        return pltpu.make_async_copy(
            weight_hbm.at[part, span, :], weight.at[part, span, :], weight_sem.at[piece, part]
        )

    own = [
        pltpu.make_async_copy(
            tokens.at[:, pl.ds(piece * cut, cut)], blocks.at[piece, z], token_sem.at[piece]
        )
        for piece in range(PIECES)
    ]
    small = [
        pltpu.make_async_copy(source, target, small_sem.at[index])
        for index, (source, target) in enumerate(
            ((grad_hbm, grad_out), (feat_hbm, feat_taps), (inner_hbm, inner_taps))
        )
    ]
    for copy in own + small:
        copy.start()
    for piece in range(PIECES):
        for part in range(3):
            weight_copy(piece, part).start()

    has_before, has_after = ctx > 0, ctx < n_ctx - 1
    barrier = pltpu.get_barrier_semaphore()

    def each_peer(act):
        def visit(index, carry):
            far = n - 1 - index

            @pl.when(z + far < n)
            def _():
                act(z + far)

            @pl.when(z >= far)
            def _():
                act(z - far)

            return carry

        lax.fori_loop(0, n - 1, visit, 0)

    def greet(here, axis, index):
        @pl.when(here)
        def _():
            pl.semaphore_signal(barrier, inc=1, device_id={axis: index}, device_id_type=MESH)

    def greet_peer(peer):
        pl.semaphore_signal(barrier, inc=1, device_id={"tp": peer}, device_id_type=MESH)

    each_peer(greet_peer)
    greet(has_before, "ctx", ctx - 1)
    greet(has_after, "ctx", ctx + 1)

    for copy in own + small:
        copy.wait()
    grads[0:total, :] = grad_out[...].astype(F32)
    grad_edge[...] = grads[0:HALO, :]

    peers = n - 1 + has_before.astype(jnp.int32) + has_after.astype(jnp.int32)
    pl.semaphore_wait(barrier, peers)

    def gather_to(piece, block, peer):
        return pltpu.make_async_remote_copy(
            src_ref=blocks.at[piece, block],
            dst_ref=blocks.at[piece, block],
            send_sem=gather_send.at[piece, peer],
            recv_sem=gather_recv.at[piece, block],
            device_id={"tp": peer},
            device_id_type=MESH,
        )

    for piece in range(PIECES):
        each_peer(lambda peer: gather_to(piece, z, peer).start())

    grad_copy = pltpu.make_async_remote_copy(
        src_ref=grad_edge,
        dst_ref=grad_halo,
        send_sem=halo_send.at[0],
        recv_sem=halo_recv.at[0],
        device_id={"ctx": ctx - 1},
        device_id_type=MESH,
    )

    @pl.when(has_before)
    def _():
        grad_copy.start()

    for piece in range(PIECES):
        each_peer(lambda peer: gather_to(piece, peer, peer).wait_recv())
        for block in range(n):
            stack[block * rows : (block + 1) * rows, :] = blocks[piece, block].astype(F32)
        left_side = stack[...].astype(BF16)
        for part in range(3):
            weight_copy(piece, part).wait()
            product = jnp.dot(
                left_side,
                weight[part, piece * cut : (piece + 1) * cut, :],
                preferred_element_type=F32,
            )
            if piece == 0:
                ext[part, HALO : HALO + total, :] = product
            else:
                ext[part, HALO : HALO + total, :] += product

    edge[0] = ext[:, HALO : 2 * HALO, :]
    edge[1] = ext[:, total : total + HALO, :]

    def edge_copy(side, target):
        return pltpu.make_async_remote_copy(
            src_ref=edge.at[side],
            dst_ref=halo.at[side],
            send_sem=halo_send.at[1 + side],
            recv_sem=halo_recv.at[1 + side],
            device_id={"ctx": target},
            device_id_type=MESH,
        )

    first_rows = edge_copy(0, ctx - 1)
    last_rows = edge_copy(1, ctx + 1)

    @pl.when(has_before)
    def _():
        first_rows.start()

    @pl.when(has_after)
    def _():
        last_rows.start()

    @pl.when(has_after)
    def _():
        grad_copy.wait_recv()
        grads[total : total + HALO, :] = grad_halo[...]
        first_rows.wait_recv()
        ext[:, HALO + total :, :] = halo[0]

    @pl.when(ctx == n_ctx - 1)
    def _():
        grads[total : total + HALO, :] = jnp.zeros((HALO, channels), F32)
        ext[:, HALO + total :, :] = jnp.zeros((3, HALO, channels), F32)

    @pl.when(has_before)
    def _():
        last_rows.wait_recv()
        ext[:, 0:HALO, :] = halo[1]

    @pl.when(ctx == 0)
    def _():
        ext[:, 0:HALO, :] = jnp.zeros((3, HALO, channels), F32)

    long = total + HALO
    lanes = 128

    def channel_step(index, carry):
        at = pl.ds(pl.multiple_of(index * lanes, lanes), lanes)

        def conv(part, start):
            terms = feat_taps[part, 0:1, at] * ext[part, start : start + long, at]
            for tap in range(1, 3):
                terms += (
                    feat_taps[part, tap : tap + 1, at]
                    * ext[part, start - tap : start - tap + long, at]
                )
            return terms

        query = conv(0, HALO)
        dinner[0:long, :] = grads[:, at] * query
        key = conv(1, 2)
        value = conv(2, 2)
        mix[0:long, :] = key * value
        dfeat[1, 0:long, :] = value
        dfeat[2, 0:long, :] = key
        inner = inner_taps[0:1, at] * mix[6 : 6 + long, :]
        for tap in range(1, 7):
            inner += inner_taps[tap : tap + 1, at] * mix[6 - tap : 6 - tap + long, :]
        gated[:, at] = (query * inner)[0:total].astype(BF16)
        dfeat[0, 0:long, :] = grads[:, at] * inner
        dmix = inner_taps[0:1, at] * dinner[0:long, :]
        for tap in range(1, 7):
            dmix += inner_taps[tap : tap + 1, at] * dinner[tap : tap + long, :]
        dkey = dmix * dfeat[1, 6 : 6 + long, :]
        dvalue = dmix * dfeat[2, 6 : 6 + long, :]
        dfeat[1, 0:long, :] = dkey
        dfeat[2, 0:long, :] = dvalue
        for part in range(3):
            series = feat_taps[part, 0:1, at] * dfeat[part, 0:total, :]
            for tap in range(1, 3):
                series += feat_taps[part, tap : tap + 1, at] * dfeat[part, tap : tap + total, :]
            dproj[part, :, at] = series.astype(BF16)
        return carry

    tail = jnp.zeros((HALO, lanes), F32)
    mix[long:, :] = tail
    dinner[long:, :] = tail
    for part in range(3):
        dfeat[part, long:, :] = tail
    lax.fori_loop(0, channels // lanes, channel_step, 0)

    def scatter_to(piece, slot, peer):
        return pltpu.make_async_remote_copy(
            src_ref=outgoing.at[piece, peer],
            dst_ref=incoming.at[piece, slot],
            send_sem=scatter_send.at[piece, peer],
            recv_sem=scatter_recv.at[piece, slot],
            device_id={"tp": peer},
            device_id_type=MESH,
        )

    for piece in range(PIECES):
        share = jnp.zeros((total, cut), F32)
        for part in range(3):
            share += lax.dot_general(
                dproj[part],
                weight[part, piece * cut : (piece + 1) * cut, :],
                (((1,), (1,)), ((), ())),
                preferred_element_type=F32,
            )
        for block in range(n):
            outgoing[piece, block] = share[block * rows : (block + 1) * rows].astype(BF16)
        each_peer(lambda peer: scatter_to(piece, z, peer).start())

    for piece in range(PIECES):
        incoming[piece, z] = outgoing[piece, z]
        each_peer(lambda peer: scatter_to(piece, peer, peer).wait_recv())
        summed = incoming[piece, 0].astype(F32)
        for block in range(1, n):
            summed += incoming[piece, block].astype(F32)
        grad_tokens[:, piece * cut : (piece + 1) * cut] = summed.astype(BF16)

    @pl.when(has_before)
    def _():
        grad_copy.wait_send()
        first_rows.wait_send()

    @pl.when(has_after)
    def _():
        last_rows.wait_send()

    for piece in range(PIECES):

        def drain(peer):
            gather_to(piece, z, peer).wait_send()
            scatter_to(piece, z, peer).wait_send()

        each_peer(drain)


def local(n, n_ctx, tokens, proj_weight, feat_taps, inner_taps, grad_out):
    rows, width = tokens.shape
    total, channels = grad_out.shape
    cut = width // PIECES
    weight = jnp.transpose(proj_weight, (1, 0, 2))
    vmem = pl.BlockSpec(memory_space=pltpu.VMEM)
    dma = pltpu.SemaphoreType.DMA
    long = total + 2 * HALO
    return pl.pallas_call(
        functools.partial(kernel, n, n_ctx),
        out_shape=(
            jax.ShapeDtypeStruct((total, channels), BF16),
            jax.ShapeDtypeStruct((rows, width), BF16),
        ),
        in_specs=[pl.BlockSpec(memory_space=pl.ANY)] * 5,
        out_specs=(vmem, vmem),
        scratch_shapes=[
            pltpu.VMEM(feat_taps.shape, F32),
            pltpu.VMEM(inner_taps.shape, F32),
            pltpu.VMEM((total, channels), BF16),
            pltpu.VMEM((3, width, channels), BF16),
            pltpu.VMEM((PIECES, n, rows, cut), BF16),
            pltpu.VMEM((total, cut), F32),
            pltpu.VMEM((3, long, channels), F32),
            pltpu.VMEM((total + HALO, channels), F32),
            pltpu.VMEM((long, 128), F32),
            pltpu.VMEM((long, 128), F32),
            pltpu.VMEM((3, long, 128), F32),
            pltpu.VMEM((3, total, channels), BF16),
            pltpu.VMEM((2, 3, HALO, channels), F32),
            pltpu.VMEM((2, 3, HALO, channels), F32),
            pltpu.VMEM((HALO, channels), F32),
            pltpu.VMEM((HALO, channels), F32),
            pltpu.VMEM((PIECES, n, rows, cut), BF16),
            pltpu.VMEM((PIECES, n, rows, cut), BF16),
            dma((PIECES, 3)),
            dma((PIECES, n)),
            dma((PIECES, n)),
            dma((PIECES, n)),
            dma((PIECES, n)),
            dma((3,)),
            dma((3,)),
            dma((PIECES,)),
            dma((3,)),
        ],
        compiler_params=pltpu.CompilerParams(
            collective_id=0, has_side_effects=True, vmem_limit_bytes=50 * 1024 * 1024
        ),
        cost_estimate=pl.CostEstimate(
            flops=4 * total * width * 3 * channels,
            bytes_accessed=6 * width * channels,
            transcendentals=0,
        ),
    )(tokens, weight, feat_taps, inner_taps, grad_out)


def solution(mesh):
    in_specs = (
        P(("ctx", "tp"), None),
        P(None, None, "tp"),
        P(None, None, "tp"),
        P(None, "tp"),
        P("ctx", "tp"),
    )
    out_specs = (P("ctx", "tp"), P(("ctx", "tp"), None))
    body = functools.partial(local, mesh.shape["tp"], mesh.shape["ctx"])
    return jax.shard_map(
        body, mesh=mesh, in_specs=in_specs, out_specs=out_specs, check_vma=False
    )
```

```python
import functools

import jax
import jax.numpy as jnp
from jax import lax
from jax.experimental import pallas as pl
from jax.experimental.pallas import tpu as pltpu
from jax.sharding import PartitionSpec as P

MESH = pl.DeviceIdType.MESH
F32 = jnp.float32
BF16 = jnp.bfloat16
PIECES = 8
GROUPS = ((0, 1), (2, 3), (4, 5), (6,), (7,))
HALO = 8


def kernel(
    n,
    n_ctx,
    tokens,
    weight_hbm,
    feat_hbm,
    inner_hbm,
    grad_hbm,
    gated,
    grad_tokens,
    feat_taps,
    inner_taps,
    grad_out,
    weight,
    blocks,
    stack,
    ext,
    grads,
    mix,
    dinner,
    dfeat,
    dproj,
    edge,
    halo,
    grad_edge,
    grad_halo,
    outgoing,
    incoming,
    relay,
    summed,
    weight_sem,
    gather_recv,
    gather_send,
    forward_send,
    relay_recv,
    scatter_recv,
    scatter_send,
    halo_send,
    halo_recv,
    token_sem,
    small_sem,
):
    z = lax.axis_index("tp")
    ctx = lax.axis_index("ctx")
    rows, width = tokens.shape
    total, channels = gated.shape
    cut = width // PIECES

    def weight_copy(piece, part):
        span = pl.ds(piece * cut, cut)
        return pltpu.make_async_copy(
            weight_hbm.at[part, span, :], weight.at[part, span, :], weight_sem.at[piece, part]
        )

    own = [
        pltpu.make_async_copy(
            tokens.at[:, pl.ds(piece * cut, cut)], blocks.at[piece, z], token_sem.at[piece]
        )
        for piece in range(PIECES)
    ]
    small = [
        pltpu.make_async_copy(source, target, small_sem.at[index])
        for index, (source, target) in enumerate(
            ((grad_hbm, grad_out), (feat_hbm, feat_taps), (inner_hbm, inner_taps))
        )
    ]
    for copy in own + small:
        copy.start()
    for piece in range(PIECES):
        for part in range(3):
            weight_copy(piece, part).start()

    has_before, has_after = ctx > 0, ctx < n_ctx - 1
    barrier = pltpu.get_barrier_semaphore()

    def each_peer(act):
        def visit(index, carry):
            far = n - 1 - index

            @pl.when(z + far < n)
            def _():
                act(z + far)

            @pl.when(z >= far)
            def _():
                act(z - far)

            return carry

        lax.fori_loop(0, n - 1, visit, 0)

    mate = z + 1 - 2 * lax.rem(z, 2)
    even = lax.rem(z, 2) == 0

    def faces(peer):
        parity = lax.rem(peer, 2)
        return ((peer > z) & (parity == 0)) | ((peer < z) & (parity == 1))

    def is_relay_for(peer):
        return (even & (peer < z)) | (jnp.logical_not(even) & (peer > z))

    def greet(here, axis, index):
        @pl.when(here)
        def _():
            pl.semaphore_signal(barrier, inc=1, device_id={axis: index}, device_id_type=MESH)

    def greet_peer(peer):
        pl.semaphore_signal(barrier, inc=1, device_id={"tp": peer}, device_id_type=MESH)

    each_peer(greet_peer)
    greet(has_before, "ctx", ctx - 1)
    greet(has_after, "ctx", ctx + 1)

    for copy in own + small:
        copy.wait()
    grads[0:total, :] = grad_out[...].astype(F32)
    grad_edge[...] = grads[0:HALO, :]

    peers = n - 1 + has_before.astype(jnp.int32) + has_after.astype(jnp.int32)
    pl.semaphore_wait(barrier, peers)

    def gather_to(piece, block, peer):
        return pltpu.make_async_remote_copy(
            src_ref=blocks.at[piece, block],
            dst_ref=blocks.at[piece, block],
            send_sem=gather_send.at[piece, peer],
            recv_sem=gather_recv.at[piece, block],
            device_id={"tp": peer},
            device_id_type=MESH,
        )

    def forward_to_mate(piece, block):
        return pltpu.make_async_remote_copy(
            src_ref=blocks.at[piece, block],
            dst_ref=blocks.at[piece, block],
            send_sem=forward_send.at[piece, block],
            recv_sem=gather_recv.at[piece, block],
            device_id={"tp": mate},
            device_id_type=MESH,
        )

    def spread(piece):
        def send(peer):
            @pl.when((peer == mate) | faces(peer))
            def _():
                gather_to(piece, z, peer).start()

        each_peer(send)

    for piece in range(PIECES):
        spread(piece)

    grad_copy = pltpu.make_async_remote_copy(
        src_ref=grad_edge,
        dst_ref=grad_halo,
        send_sem=halo_send.at[0],
        recv_sem=halo_recv.at[0],
        device_id={"ctx": ctx - 1},
        device_id_type=MESH,
    )

    @pl.when(has_before)
    def _():
        grad_copy.start()

    def collect(piece):
        def take(peer):
            @pl.when(is_relay_for(peer))
            def _():
                gather_to(piece, peer, peer).wait_recv()
                forward_to_mate(piece, peer).start()

        def take_rest(peer):
            @pl.when(jnp.logical_not(is_relay_for(peer)))
            def _():
                gather_to(piece, peer, peer).wait_recv()

        each_peer(take)
        each_peer(take_rest)

    for group in GROUPS:
        for place, piece in enumerate(group):
            collect(piece)
            for block in range(n):
                stack[block * rows : (block + 1) * rows, place * cut : (place + 1) * cut] = (
                    blocks[piece, block].astype(F32)
                )
            for part in range(3):
                weight_copy(piece, part).wait()
        depth = len(group) * cut
        left_side = stack[:, 0:depth].astype(BF16)
        first = group[0] * cut
        for part in range(3):
            product = jnp.dot(
                left_side,
                weight[part, first : first + depth, :],
                preferred_element_type=F32,
            )
            if group[0] == 0:
                ext[part, HALO : HALO + total, :] = product
            else:
                ext[part, HALO : HALO + total, :] += product

    edge[0] = ext[:, HALO : 2 * HALO, :]
    edge[1] = ext[:, total : total + HALO, :]

    def edge_copy(side, target):
        return pltpu.make_async_remote_copy(
            src_ref=edge.at[side],
            dst_ref=halo.at[side],
            send_sem=halo_send.at[1 + side],
            recv_sem=halo_recv.at[1 + side],
            device_id={"ctx": target},
            device_id_type=MESH,
        )

    first_rows = edge_copy(0, ctx - 1)
    last_rows = edge_copy(1, ctx + 1)

    @pl.when(has_before)
    def _():
        first_rows.start()

    @pl.when(has_after)
    def _():
        last_rows.start()

    @pl.when(has_after)
    def _():
        grad_copy.wait_recv()
        grads[total : total + HALO, :] = grad_halo[...]
        first_rows.wait_recv()
        ext[:, HALO + total :, :] = halo[0]

    @pl.when(ctx == n_ctx - 1)
    def _():
        grads[total : total + HALO, :] = jnp.zeros((HALO, channels), F32)
        ext[:, HALO + total :, :] = jnp.zeros((3, HALO, channels), F32)

    @pl.when(has_before)
    def _():
        last_rows.wait_recv()
        ext[:, 0:HALO, :] = halo[1]

    @pl.when(ctx == 0)
    def _():
        ext[:, 0:HALO, :] = jnp.zeros((3, HALO, channels), F32)

    long = total + HALO
    lanes = 128

    def channel_step(index, carry):
        at = pl.ds(pl.multiple_of(index * lanes, lanes), lanes)

        def conv(part, start):
            terms = feat_taps[part, 0:1, at] * ext[part, start : start + long, at]
            for tap in range(1, 3):
                terms += (
                    feat_taps[part, tap : tap + 1, at]
                    * ext[part, start - tap : start - tap + long, at]
                )
            return terms

        query = conv(0, HALO)
        dinner[0:long, :] = grads[:, at] * query
        key = conv(1, 2)
        value = conv(2, 2)
        mix[0:long, :] = key * value
        dfeat[1, 0:long, :] = value
        dfeat[2, 0:long, :] = key
        inner = inner_taps[0:1, at] * mix[6 : 6 + long, :]
        for tap in range(1, 7):
            inner += inner_taps[tap : tap + 1, at] * mix[6 - tap : 6 - tap + long, :]
        gated[:, at] = (query * inner)[0:total].astype(BF16)
        dfeat[0, 0:long, :] = grads[:, at] * inner
        dmix = inner_taps[0:1, at] * dinner[0:long, :]
        for tap in range(1, 7):
            dmix += inner_taps[tap : tap + 1, at] * dinner[tap : tap + long, :]
        dkey = dmix * dfeat[1, 6 : 6 + long, :]
        dvalue = dmix * dfeat[2, 6 : 6 + long, :]
        dfeat[1, 0:long, :] = dkey
        dfeat[2, 0:long, :] = dvalue
        for part in range(3):
            series = feat_taps[part, 0:1, at] * dfeat[part, 0:total, :]
            for tap in range(1, 3):
                series += feat_taps[part, tap : tap + 1, at] * dfeat[part, tap : tap + total, :]
            dproj[part, :, at] = series.astype(BF16)
        return carry

    tail = jnp.zeros((HALO, lanes), F32)
    mix[long:, :] = tail
    dinner[long:, :] = tail
    for part in range(3):
        dfeat[part, long:, :] = tail
    lax.fori_loop(0, channels // lanes, channel_step, 0)

    def scatter_to(piece, slot, peer):
        return pltpu.make_async_remote_copy(
            src_ref=outgoing.at[piece, peer],
            dst_ref=incoming.at[piece, slot],
            send_sem=scatter_send.at[piece, peer],
            recv_sem=scatter_recv.at[piece, slot],
            device_id={"tp": peer},
            device_id_type=MESH,
        )

    def relay_to_mate(piece, block):
        return pltpu.make_async_remote_copy(
            src_ref=outgoing.at[piece, block],
            dst_ref=relay.at[piece, block],
            send_sem=scatter_send.at[piece, block],
            recv_sem=relay_recv.at[piece, block],
            device_id={"tp": mate},
            device_id_type=MESH,
        )

    def combine(piece):
        def add(peer):
            @pl.when(is_relay_for(peer))
            def _():
                relay_to_mate(piece, peer).wait_recv()
                outgoing[piece, peer] = (
                    outgoing[piece, peer].astype(F32) + relay[piece, peer].astype(F32)
                ).astype(BF16)
                scatter_to(piece, z, peer).start()

        each_peer(add)

    for piece in range(PIECES):
        share = jnp.zeros((total, cut), F32)
        for part in range(3):
            share += lax.dot_general(
                dproj[part],
                weight[part, piece * cut : (piece + 1) * cut, :],
                (((1,), (1,)), ((), ())),
                preferred_element_type=F32,
            )
        for block in range(n):
            outgoing[piece, block] = share[block * rows : (block + 1) * rows].astype(BF16)

        def hand_over(peer):
            @pl.when(jnp.logical_not(is_relay_for(peer)) & (peer != mate))
            def _():
                relay_to_mate(piece, peer).start()

        each_peer(hand_over)
        scatter_to(piece, z, mate).start()
        if piece > 0:
            combine(piece - 1)
    combine(PIECES - 1)

    for piece in range(PIECES):
        scatter_to(piece, mate, mate).wait_recv()
        summed[...] = outgoing[piece, z].astype(F32) + incoming[piece, mate].astype(F32)

        def gain(peer):
            @pl.when(faces(peer) & (peer != mate))
            def _():
                scatter_to(piece, peer, peer).wait_recv()
                summed[...] += incoming[piece, peer].astype(F32)

        each_peer(gain)
        grad_tokens[:, piece * cut : (piece + 1) * cut] = summed[...].astype(BF16)

    @pl.when(has_before)
    def _():
        grad_copy.wait_send()
        first_rows.wait_send()

    @pl.when(has_after)
    def _():
        last_rows.wait_send()

    for piece in range(PIECES):

        def drain(peer):
            @pl.when((peer == mate) | faces(peer))
            def _():
                gather_to(piece, z, peer).wait_send()

            @pl.when(is_relay_for(peer))
            def _():
                forward_to_mate(piece, peer).wait_send()

            scatter_to(piece, z, peer).wait_send()

        each_peer(drain)


def local(n, n_ctx, tokens, proj_weight, feat_taps, inner_taps, grad_out):
    rows, width = tokens.shape
    total, channels = grad_out.shape
    cut = width // PIECES
    weight = jnp.transpose(proj_weight, (1, 0, 2))
    vmem = pl.BlockSpec(memory_space=pltpu.VMEM)
    dma = pltpu.SemaphoreType.DMA
    long = total + 2 * HALO
    return pl.pallas_call(
        functools.partial(kernel, n, n_ctx),
        out_shape=(
            jax.ShapeDtypeStruct((total, channels), BF16),
            jax.ShapeDtypeStruct((rows, width), BF16),
        ),
        in_specs=[pl.BlockSpec(memory_space=pltpu.HBM)] * 5,
        out_specs=(vmem, vmem),
        scratch_shapes=[
            pltpu.VMEM(feat_taps.shape, F32),
            pltpu.VMEM(inner_taps.shape, F32),
            pltpu.VMEM((total, channels), BF16),
            pltpu.VMEM((3, width, channels), BF16),
            pltpu.VMEM((PIECES, n, rows, cut), BF16),
            pltpu.VMEM((total, 2 * cut), F32),
            pltpu.VMEM((3, long, channels), F32),
            pltpu.VMEM((total + HALO, channels), F32),
            pltpu.VMEM((long, 128), F32),
            pltpu.VMEM((long, 128), F32),
            pltpu.VMEM((3, long, 128), F32),
            pltpu.VMEM((3, total, channels), BF16),
            pltpu.VMEM((2, 3, HALO, channels), F32),
            pltpu.VMEM((2, 3, HALO, channels), F32),
            pltpu.VMEM((HALO, channels), F32),
            pltpu.VMEM((HALO, channels), F32),
            pltpu.VMEM((PIECES, n, rows, cut), BF16),
            pltpu.VMEM((PIECES, n, rows, cut), BF16),
            pltpu.VMEM((PIECES, n, rows, cut), BF16),
            pltpu.VMEM((rows, cut), F32),
            dma((PIECES, 3)),
            dma((PIECES, n)),
            dma((PIECES, n)),
            dma((PIECES, n)),
            dma((PIECES, n)),
            dma((PIECES, n)),
            dma((PIECES, n)),
            dma((3,)),
            dma((3,)),
            dma((PIECES,)),
            dma((3,)),
        ],
        compiler_params=pltpu.CompilerParams(
            collective_id=0, has_side_effects=True, vmem_limit_bytes=50 * 1024 * 1024
        ),
        cost_estimate=pl.CostEstimate(
            flops=4 * total * width * 3 * channels,
            bytes_accessed=6 * width * channels,
            transcendentals=0,
        ),
    )(tokens, weight, feat_taps, inner_taps, grad_out)


def solution(mesh):
    in_specs = (
        P(("ctx", "tp"), None),
        P(None, None, "tp"),
        P(None, None, "tp"),
        P(None, "tp"),
        P("ctx", "tp"),
    )
    out_specs = (P("ctx", "tp"), P(("ctx", "tp"), None))
    body = functools.partial(local, mesh.shape["tp"], mesh.shape["ctx"])
    return jax.shard_map(
        body, mesh=mesh, in_specs=in_specs, out_specs=out_specs, check_vma=False
    )
```

```python
import functools

import jax
import jax.numpy as jnp
from jax import lax
from jax.experimental import pallas as pl
from jax.experimental.pallas import tpu as pltpu
from jax.sharding import PartitionSpec as P

MESH = pl.DeviceIdType.MESH
F32 = jnp.float32
BF16 = jnp.bfloat16
PIECES = 8
GROUPS = ((0, 1), (2, 3), (4, 5), (6,), (7,))
HALO = 8


def kernel(
    n,
    n_ctx,
    tokens,
    weight_hbm,
    feat_hbm,
    inner_hbm,
    grad_hbm,
    gated_hbm,
    grad_tokens_hbm,
    gated,
    grad_tokens,
    feat_taps,
    inner_taps,
    grad_out,
    weight,
    blocks,
    stack,
    ext,
    grads,
    mix,
    dinner,
    dfeat,
    dproj,
    edge,
    halo,
    grad_edge,
    grad_halo,
    outgoing,
    incoming,
    relay,
    summed,
    weight_sem,
    gather_recv,
    gather_send,
    forward_send,
    relay_recv,
    scatter_recv,
    scatter_send,
    halo_send,
    halo_recv,
    token_sem,
    small_sem,
):
    z = lax.axis_index("tp")
    ctx = lax.axis_index("ctx")
    rows, width = tokens.shape
    total, channels = gated.shape
    edge_rows = 2 * HALO
    cut = width // PIECES

    def weight_copy(piece, part):
        span = pl.ds(piece * cut, cut)
        return pltpu.make_async_copy(
            weight_hbm.at[part, span, :], weight.at[part, span, :], weight_sem.at[piece, part]
        )

    own = [
        pltpu.make_async_copy(
            tokens.at[:, pl.ds(piece * cut, cut)], blocks.at[piece, z], token_sem.at[piece]
        )
        for piece in range(PIECES)
    ]
    small = [
        pltpu.make_async_copy(source, target, small_sem.at[index])
        for index, (source, target) in enumerate(
            ((grad_hbm, grad_out), (feat_hbm, feat_taps), (inner_hbm, inner_taps))
        )
    ]
    for copy in own + small:
        copy.start()
    for piece in range(PIECES):
        for part in range(3):
            weight_copy(piece, part).start()

    has_before, has_after = ctx > 0, ctx < n_ctx - 1
    barrier = pltpu.get_barrier_semaphore()

    def each_peer(act):
        def visit(index, carry):
            far = n - 1 - index

            @pl.when(z + far < n)
            def _():
                act(z + far)

            @pl.when(z >= far)
            def _():
                act(z - far)

            return carry

        lax.fori_loop(0, n - 1, visit, 0)

    mate = z + 1 - 2 * lax.rem(z, 2)
    even = lax.rem(z, 2) == 0

    def faces(peer):
        parity = lax.rem(peer, 2)
        return ((peer > z) & (parity == 0)) | ((peer < z) & (parity == 1))

    def is_relay_for(peer):
        return (even & (peer < z)) | (jnp.logical_not(even) & (peer > z))

    def greet(here, axis, index):
        @pl.when(here)
        def _():
            pl.semaphore_signal(barrier, inc=1, device_id={axis: index}, device_id_type=MESH)

    def greet_peer(peer):
        pl.semaphore_signal(barrier, inc=1, device_id={"tp": peer}, device_id_type=MESH)

    each_peer(greet_peer)
    greet(has_before, "ctx", ctx - 1)
    greet(has_after, "ctx", ctx + 1)

    peers = n - 1 + has_before.astype(jnp.int32) + has_after.astype(jnp.int32)
    pl.semaphore_wait(barrier, peers)

    def send_own(piece, peer):
        return pltpu.make_async_remote_copy(
            src_ref=tokens.at[:, pl.ds(piece * cut, cut)],
            dst_ref=blocks.at[piece, z],
            send_sem=gather_send.at[piece, peer],
            recv_sem=gather_recv.at[piece, z],
            device_id={"tp": peer},
            device_id_type=MESH,
        )

    def gather_to(piece, block, peer):
        return pltpu.make_async_remote_copy(
            src_ref=blocks.at[piece, block],
            dst_ref=blocks.at[piece, block],
            send_sem=gather_send.at[piece, peer],
            recv_sem=gather_recv.at[piece, block],
            device_id={"tp": peer},
            device_id_type=MESH,
        )

    def forward_to_mate(piece, block):
        return pltpu.make_async_remote_copy(
            src_ref=blocks.at[piece, block],
            dst_ref=blocks.at[piece, block],
            send_sem=forward_send.at[piece, block],
            recv_sem=gather_recv.at[piece, block],
            device_id={"tp": mate},
            device_id_type=MESH,
        )

    def spread(piece):
        def send(peer):
            @pl.when((peer == mate) | faces(peer))
            def _():
                send_own(piece, peer).start()

        each_peer(send)

    for piece in range(PIECES):
        spread(piece)

    for copy in own + small:
        copy.wait()
    grads[0:total, :] = grad_out[...].astype(F32)
    grad_edge[...] = grads[0:HALO, :]

    grad_copy = pltpu.make_async_remote_copy(
        src_ref=grad_edge,
        dst_ref=grad_halo,
        send_sem=halo_send.at[0],
        recv_sem=halo_recv.at[0],
        device_id={"ctx": ctx - 1},
        device_id_type=MESH,
    )

    @pl.when(has_before)
    def _():
        grad_copy.start()

    def collect(piece):
        def take(peer):
            @pl.when(is_relay_for(peer))
            def _():
                gather_to(piece, peer, peer).wait_recv()
                forward_to_mate(piece, peer).start()

        def take_rest(peer):
            @pl.when(jnp.logical_not(is_relay_for(peer)))
            def _():
                gather_to(piece, peer, peer).wait_recv()

        each_peer(take)
        each_peer(take_rest)

    for group in GROUPS:
        for place, piece in enumerate(group):
            collect(piece)
            for block in range(n):
                stack[block * rows : (block + 1) * rows, place * cut : (place + 1) * cut] = (
                    blocks[piece, block].astype(F32)
                )
            for part in range(3):
                weight_copy(piece, part).wait()
        depth = len(group) * cut
        left_side = stack[:, 0:depth].astype(BF16)
        first = group[0] * cut
        for part in range(3):
            product = jnp.dot(
                left_side,
                weight[part, first : first + depth, :],
                preferred_element_type=F32,
            )
            if group[0] == 0:
                ext[part, HALO : HALO + total, :] = product
            else:
                ext[part, HALO : HALO + total, :] += product

    edge[0] = ext[:, HALO : 2 * HALO, :]
    edge[1] = ext[:, total : total + HALO, :]

    def edge_copy(side, target):
        return pltpu.make_async_remote_copy(
            src_ref=edge.at[side],
            dst_ref=halo.at[side],
            send_sem=halo_send.at[1 + side],
            recv_sem=halo_recv.at[1 + side],
            device_id={"ctx": target},
            device_id_type=MESH,
        )

    first_rows = edge_copy(0, ctx - 1)
    last_rows = edge_copy(1, ctx + 1)

    @pl.when(has_before)
    def _():
        first_rows.start()

    @pl.when(has_after)
    def _():
        last_rows.start()

    for scratch in (mix, dinner, dfeat):
        scratch[...] = jnp.zeros(scratch.shape, F32)

    def convolve(top, count, at):
        long = count + HALO

        def conv(part, start):
            terms = feat_taps[part, 0:1, at] * ext[part, start : start + long, at]
            for tap in range(1, 3):
                terms += (
                    feat_taps[part, tap : tap + 1, at]
                    * ext[part, start - tap : start - tap + long, at]
                )
            return terms

        cotangent = grads[top : top + long, at]
        query = conv(0, top + HALO)
        dinner[0:long, at] = cotangent * query
        key = conv(1, top + 2)
        value = conv(2, top + 2)
        mix[0:long, at] = key * value
        dfeat[1, 0:long, at] = value
        dfeat[2, 0:long, at] = key
        inner = inner_taps[0:1, at] * mix[6 : 6 + long, at]
        for tap in range(1, 7):
            inner += inner_taps[tap : tap + 1, at] * mix[6 - tap : 6 - tap + long, at]
        gated[top : top + count, at] = (query * inner)[0:count].astype(BF16)
        dfeat[0, 0:long, at] = cotangent * inner
        dmix = inner_taps[0:1, at] * dinner[0:long, at]
        for tap in range(1, 7):
            dmix += inner_taps[tap : tap + 1, at] * dinner[tap : tap + long, at]
        dkey = dmix * dfeat[1, 6 : 6 + long, at]
        dvalue = dmix * dfeat[2, 6 : 6 + long, at]
        dfeat[1, 0:long, at] = dkey
        dfeat[2, 0:long, at] = dvalue
        for part in range(3):
            series = feat_taps[part, 0:1, at] * dfeat[part, 0:count, at]
            for tap in range(1, 3):
                series += feat_taps[part, tap : tap + 1, at] * dfeat[part, tap : tap + count, at]
            dproj[part, top : top + count, at] = series.astype(BF16)

    def each_lanes(act):
        def visit(index, carry):
            act(pl.ds(pl.multiple_of(index * 128, 128), 128))
            return carry

        lax.fori_loop(0, channels // 128, visit, 0)

    each_lanes(lambda at: convolve(edge_rows, total - 2 * edge_rows, at))

    @pl.when(has_after)
    def _():
        grad_copy.wait_recv()
        grads[total : total + HALO, :] = grad_halo[...]
        first_rows.wait_recv()
        ext[:, HALO + total :, :] = halo[0]

    @pl.when(ctx == n_ctx - 1)
    def _():
        grads[total : total + HALO, :] = jnp.zeros((HALO, channels), F32)
        ext[:, HALO + total :, :] = jnp.zeros((3, HALO, channels), F32)

    @pl.when(has_before)
    def _():
        last_rows.wait_recv()
        ext[:, 0:HALO, :] = halo[1]

    @pl.when(ctx == 0)
    def _():
        ext[:, 0:HALO, :] = jnp.zeros((3, HALO, channels), F32)

    def edges(at):
        convolve(0, edge_rows, at)
        convolve(total - edge_rows, edge_rows, at)

    each_lanes(edges)
    gated_copy = pltpu.make_async_copy(gated, gated_hbm, small_sem.at[3])
    gated_copy.start()

    def scatter_to(piece, slot, peer):
        return pltpu.make_async_remote_copy(
            src_ref=outgoing.at[piece, peer],
            dst_ref=incoming.at[piece, slot],
            send_sem=scatter_send.at[piece, peer],
            recv_sem=scatter_recv.at[piece, slot],
            device_id={"tp": peer},
            device_id_type=MESH,
        )

    def relay_to_mate(piece, block):
        return pltpu.make_async_remote_copy(
            src_ref=outgoing.at[piece, block],
            dst_ref=relay.at[piece, block],
            send_sem=scatter_send.at[piece, block],
            recv_sem=relay_recv.at[piece, block],
            device_id={"tp": mate},
            device_id_type=MESH,
        )

    def combine(piece):
        def add(peer):
            @pl.when(is_relay_for(peer))
            def _():
                relay_to_mate(piece, peer).wait_recv()
                outgoing[piece, peer] = (
                    outgoing[piece, peer].astype(F32) + relay[piece, peer].astype(F32)
                ).astype(BF16)
                scatter_to(piece, z, peer).start()

        each_peer(add)

    for piece in range(PIECES):
        share = jnp.zeros((total, cut), F32)
        for part in range(3):
            share += lax.dot_general(
                dproj[part],
                weight[part, piece * cut : (piece + 1) * cut, :],
                (((1,), (1,)), ((), ())),
                preferred_element_type=F32,
            )
        for block in range(n):
            outgoing[piece, block] = share[block * rows : (block + 1) * rows].astype(BF16)

        def hand_over(peer):
            @pl.when(jnp.logical_not(is_relay_for(peer)) & (peer != mate))
            def _():
                relay_to_mate(piece, peer).start()

        each_peer(hand_over)
        scatter_to(piece, z, mate).start()
        if piece > 0:
            combine(piece - 1)
    combine(PIECES - 1)

    def result_copy(piece):
        return pltpu.make_async_copy(
            grad_tokens.at[piece],
            grad_tokens_hbm.at[:, pl.ds(piece * cut, cut)],
            token_sem.at[piece],
        )

    for piece in range(PIECES):
        scatter_to(piece, mate, mate).wait_recv()
        summed[...] = outgoing[piece, z].astype(F32) + incoming[piece, mate].astype(F32)

        def gain(peer):
            @pl.when(faces(peer) & (peer != mate))
            def _():
                scatter_to(piece, peer, peer).wait_recv()
                summed[...] += incoming[piece, peer].astype(F32)

        each_peer(gain)
        grad_tokens[piece] = summed[...].astype(BF16)
        result_copy(piece).start()

    @pl.when(has_before)
    def _():
        grad_copy.wait_send()
        first_rows.wait_send()

    @pl.when(has_after)
    def _():
        last_rows.wait_send()

    for piece in range(PIECES):

        def drain(peer):
            @pl.when((peer == mate) | faces(peer))
            def _():
                send_own(piece, peer).wait_send()

            @pl.when(is_relay_for(peer))
            def _():
                forward_to_mate(piece, peer).wait_send()

            scatter_to(piece, z, peer).wait_send()

        each_peer(drain)
        result_copy(piece).wait()

    gated_copy.wait()


def local(n, n_ctx, tokens, proj_weight, feat_taps, inner_taps, grad_out):
    rows, width = tokens.shape
    total, channels = grad_out.shape
    cut = width // PIECES
    weight = jnp.transpose(proj_weight, (1, 0, 2))
    anywhere = pl.BlockSpec(memory_space=pl.ANY)
    dma = pltpu.SemaphoreType.DMA
    long = total + 2 * HALO
    return pl.pallas_call(
        functools.partial(kernel, n, n_ctx),
        out_shape=(
            jax.ShapeDtypeStruct((total, channels), BF16),
            jax.ShapeDtypeStruct((rows, width), BF16),
        ),
        in_specs=[anywhere] * 5,
        out_specs=(anywhere, anywhere),
        scratch_shapes=[
            pltpu.VMEM((total, channels), BF16),
            pltpu.VMEM((PIECES, rows, cut), BF16),
            pltpu.VMEM(feat_taps.shape, F32),
            pltpu.VMEM(inner_taps.shape, F32),
            pltpu.VMEM((total, channels), BF16),
            pltpu.VMEM((3, width, channels), BF16),
            pltpu.VMEM((PIECES, n, rows, cut), BF16),
            pltpu.VMEM((total, 2 * cut), F32),
            pltpu.VMEM((3, long, channels), F32),
            pltpu.VMEM((total + HALO, channels), F32),
            pltpu.VMEM((long, channels), F32),
            pltpu.VMEM((long, channels), F32),
            pltpu.VMEM((3, long, channels), F32),
            pltpu.VMEM((3, total, channels), BF16),
            pltpu.VMEM((2, 3, HALO, channels), F32),
            pltpu.VMEM((2, 3, HALO, channels), F32),
            pltpu.VMEM((HALO, channels), F32),
            pltpu.VMEM((HALO, channels), F32),
            pltpu.VMEM((PIECES, n, rows, cut), BF16),
            pltpu.VMEM((PIECES, n, rows, cut), BF16),
            pltpu.VMEM((PIECES, n, rows, cut), BF16),
            pltpu.VMEM((rows, cut), F32),
            dma((PIECES, 3)),
            dma((PIECES, n)),
            dma((PIECES, n)),
            dma((PIECES, n)),
            dma((PIECES, n)),
            dma((PIECES, n)),
            dma((PIECES, n)),
            dma((3,)),
            dma((3,)),
            dma((PIECES,)),
            dma((4,)),
        ],
        compiler_params=pltpu.CompilerParams(
            collective_id=0, has_side_effects=True, vmem_limit_bytes=56 * 1024 * 1024
        ),
        cost_estimate=pl.CostEstimate(
            flops=4 * total * width * 3 * channels,
            bytes_accessed=6 * width * channels,
            transcendentals=0,
        ),
    )(tokens, weight, feat_taps, inner_taps, grad_out)


def solution(mesh):
    in_specs = (
        P(("ctx", "tp"), None),
        P(None, None, "tp"),
        P(None, None, "tp"),
        P(None, "tp"),
        P("ctx", "tp"),
    )
    out_specs = (P("ctx", "tp"), P(("ctx", "tp"), None))
    body = functools.partial(local, mesh.shape["tp"], mesh.shape["ctx"])
    return jax.shard_map(
        body, mesh=mesh, in_specs=in_specs, out_specs=out_specs, check_vma=False
    )
```

```python
import functools

import jax
import jax.numpy as jnp
from jax import lax
from jax.experimental import pallas as pl
from jax.experimental.pallas import tpu as pltpu
from jax.sharding import PartitionSpec as P

MESH = pl.DeviceIdType.MESH
F32 = jnp.float32
BF16 = jnp.bfloat16
PIECES = 8
GROUPS = ((0, 1), (2, 3), (4, 5), (6,), (7,))
HALO = 8


def kernel(
    n,
    n_ctx,
    tokens,
    weight_hbm,
    feat_hbm,
    inner_hbm,
    grad_hbm,
    gated_hbm,
    grad_tokens_hbm,
    gated,
    grad_tokens,
    feat_taps,
    inner_taps,
    grad_out,
    weight,
    blocks,
    stack,
    ext,
    grads,
    mix,
    dinner,
    dfeat,
    dproj,
    edge,
    halo,
    grad_edge,
    grad_halo,
    outgoing,
    incoming,
    relay,
    summed,
    weight_sem,
    gather_recv,
    gather_send,
    forward_send,
    relay_recv,
    scatter_recv,
    scatter_send,
    halo_send,
    halo_recv,
    token_sem,
    small_sem,
):
    z = lax.axis_index("tp")
    ctx = lax.axis_index("ctx")
    rows, width = tokens.shape
    total, channels = gated.shape
    edge_rows = 2 * HALO
    cut = width // PIECES

    def weight_copy(piece, part):
        span = pl.ds(piece * cut, cut)
        return pltpu.make_async_copy(
            weight_hbm.at[part, span, :], weight.at[part, span, :], weight_sem.at[piece, part]
        )

    own = [
        pltpu.make_async_copy(
            tokens.at[:, pl.ds(piece * cut, cut)], blocks.at[piece, z], token_sem.at[piece]
        )
        for piece in range(PIECES)
    ]
    small = [
        pltpu.make_async_copy(source, target, small_sem.at[index])
        for index, (source, target) in enumerate(
            ((grad_hbm, grad_out), (feat_hbm, feat_taps), (inner_hbm, inner_taps))
        )
    ]
    has_before, has_after = ctx > 0, ctx < n_ctx - 1
    barrier = pltpu.get_barrier_semaphore()

    def each_peer(act):
        def visit(index, carry):
            far = n - 1 - index

            @pl.when(z + far < n)
            def _():
                act(z + far)

            @pl.when(z >= far)
            def _():
                act(z - far)

            return carry

        if n <= 8:
            for index in range(n - 1):
                visit(index, 0)
        else:
            lax.fori_loop(0, n - 1, visit, 0)

    mate = z + 1 - 2 * lax.rem(z, 2)
    even = lax.rem(z, 2) == 0

    def faces(peer):
        parity = lax.rem(peer, 2)
        return ((peer > z) & (parity == 0)) | ((peer < z) & (parity == 1))

    def is_relay_for(peer):
        return (even & (peer < z)) | (jnp.logical_not(even) & (peer > z))

    def greet(here, axis, index):
        @pl.when(here)
        def _():
            pl.semaphore_signal(barrier, inc=1, device_id={axis: index}, device_id_type=MESH)

    def greet_peer(peer):
        pl.semaphore_signal(barrier, inc=1, device_id={"tp": peer}, device_id_type=MESH)

    each_peer(greet_peer)
    greet(has_before, "ctx", ctx - 1)
    greet(has_after, "ctx", ctx + 1)

    for copy in own + small:
        copy.start()
    for part in range(3):
        weight_copy(0, part).start()

    peers = n - 1 + has_before.astype(jnp.int32) + has_after.astype(jnp.int32)
    pl.semaphore_wait(barrier, peers)

    def send_own(piece, peer):
        return pltpu.make_async_remote_copy(
            src_ref=tokens.at[:, pl.ds(piece * cut, cut)],
            dst_ref=blocks.at[piece, z],
            send_sem=gather_send.at[piece, peer],
            recv_sem=gather_recv.at[piece, z],
            device_id={"tp": peer},
            device_id_type=MESH,
        )

    def gather_to(piece, block, peer):
        return pltpu.make_async_remote_copy(
            src_ref=blocks.at[piece, block],
            dst_ref=blocks.at[piece, block],
            send_sem=gather_send.at[piece, peer],
            recv_sem=gather_recv.at[piece, block],
            device_id={"tp": peer},
            device_id_type=MESH,
        )

    def forward_to_mate(piece, block):
        return pltpu.make_async_remote_copy(
            src_ref=blocks.at[piece, block],
            dst_ref=blocks.at[piece, block],
            send_sem=forward_send.at[piece, block],
            recv_sem=gather_recv.at[piece, block],
            device_id={"tp": mate},
            device_id_type=MESH,
        )

    def spread(piece):
        def send(peer):
            @pl.when((peer == mate) | faces(peer))
            def _():
                send_own(piece, peer).start()

        each_peer(send)

    for piece in range(PIECES):
        spread(piece)

    for piece in range(1, PIECES):
        for part in range(3):
            weight_copy(piece, part).start()

    for copy in own + small:
        copy.wait()
    grads[0:total, :] = grad_out[...].astype(F32)
    grad_edge[...] = grads[0:HALO, :]

    grad_copy = pltpu.make_async_remote_copy(
        src_ref=grad_edge,
        dst_ref=grad_halo,
        send_sem=halo_send.at[0],
        recv_sem=halo_recv.at[0],
        device_id={"ctx": ctx - 1},
        device_id_type=MESH,
    )

    @pl.when(has_before)
    def _():
        grad_copy.start()

    def collect(piece):
        def take(peer):
            @pl.when(is_relay_for(peer))
            def _():
                gather_to(piece, peer, peer).wait_recv()
                forward_to_mate(piece, peer).start()

        def take_rest(peer):
            @pl.when(jnp.logical_not(is_relay_for(peer)))
            def _():
                gather_to(piece, peer, peer).wait_recv()

        each_peer(take)
        each_peer(take_rest)

    for group in GROUPS:
        for place, piece in enumerate(group):
            collect(piece)
            for block in range(n):
                stack[block * rows : (block + 1) * rows, place * cut : (place + 1) * cut] = (
                    blocks[piece, block].astype(F32)
                )
            for part in range(3):
                weight_copy(piece, part).wait()
        depth = len(group) * cut
        left_side = stack[:, 0:depth].astype(BF16)
        first = group[0] * cut
        for part in range(3):
            product = jnp.dot(
                left_side,
                weight[part, first : first + depth, :],
                preferred_element_type=F32,
            )
            if group[0] == 0:
                ext[part, HALO : HALO + total, :] = product
            else:
                ext[part, HALO : HALO + total, :] += product

    edge[0] = ext[:, HALO : 2 * HALO, :]
    edge[1] = ext[:, total : total + HALO, :]

    def edge_copy(side, target):
        return pltpu.make_async_remote_copy(
            src_ref=edge.at[side],
            dst_ref=halo.at[side],
            send_sem=halo_send.at[1 + side],
            recv_sem=halo_recv.at[1 + side],
            device_id={"ctx": target},
            device_id_type=MESH,
        )

    first_rows = edge_copy(0, ctx - 1)
    last_rows = edge_copy(1, ctx + 1)

    @pl.when(has_before)
    def _():
        first_rows.start()

    @pl.when(has_after)
    def _():
        last_rows.start()

    for scratch in (mix, dinner, dfeat):
        scratch[...] = jnp.zeros(scratch.shape, F32)

    def convolve(top, count, at):
        long = count + HALO

        def conv(part, start):
            terms = feat_taps[part, 0:1, at] * ext[part, start : start + long, at]
            for tap in range(1, 3):
                terms += (
                    feat_taps[part, tap : tap + 1, at]
                    * ext[part, start - tap : start - tap + long, at]
                )
            return terms

        cotangent = grads[top : top + long, at]
        query = conv(0, top + HALO)
        dinner[0:long, at] = cotangent * query
        key = conv(1, top + 2)
        value = conv(2, top + 2)
        mix[0:long, at] = key * value
        dfeat[1, 0:long, at] = value
        dfeat[2, 0:long, at] = key
        inner = inner_taps[0:1, at] * mix[6 : 6 + long, at]
        for tap in range(1, 7):
            inner += inner_taps[tap : tap + 1, at] * mix[6 - tap : 6 - tap + long, at]
        gated[top : top + count, at] = (query * inner)[0:count].astype(BF16)
        dfeat[0, 0:long, at] = cotangent * inner
        dmix = inner_taps[0:1, at] * dinner[0:long, at]
        for tap in range(1, 7):
            dmix += inner_taps[tap : tap + 1, at] * dinner[tap : tap + long, at]
        dkey = dmix * dfeat[1, 6 : 6 + long, at]
        dvalue = dmix * dfeat[2, 6 : 6 + long, at]
        dfeat[1, 0:long, at] = dkey
        dfeat[2, 0:long, at] = dvalue
        for part in range(3):
            series = feat_taps[part, 0:1, at] * dfeat[part, 0:count, at]
            for tap in range(1, 3):
                series += feat_taps[part, tap : tap + 1, at] * dfeat[part, tap : tap + count, at]
            dproj[part, top : top + count, at] = series.astype(BF16)

    def each_lanes(act):
        def visit(index, carry):
            act(pl.ds(pl.multiple_of(index * 128, 128), 128))
            return carry

        lax.fori_loop(0, channels // 128, visit, 0)

    each_lanes(lambda at: convolve(edge_rows, total - 2 * edge_rows, at))

    @pl.when(has_after)
    def _():
        grad_copy.wait_recv()
        grads[total : total + HALO, :] = grad_halo[...]
        first_rows.wait_recv()
        ext[:, HALO + total :, :] = halo[0]

    @pl.when(ctx == n_ctx - 1)
    def _():
        grads[total : total + HALO, :] = jnp.zeros((HALO, channels), F32)
        ext[:, HALO + total :, :] = jnp.zeros((3, HALO, channels), F32)

    @pl.when(has_before)
    def _():
        last_rows.wait_recv()
        ext[:, 0:HALO, :] = halo[1]

    @pl.when(ctx == 0)
    def _():
        ext[:, 0:HALO, :] = jnp.zeros((3, HALO, channels), F32)

    def edges(at):
        convolve(0, edge_rows, at)
        convolve(total - edge_rows, edge_rows, at)

    each_lanes(edges)
    gated_copy = pltpu.make_async_copy(gated, gated_hbm, small_sem.at[3])
    gated_copy.start()

    def scatter_to(piece, slot, peer):
        return pltpu.make_async_remote_copy(
            src_ref=outgoing.at[piece, peer],
            dst_ref=incoming.at[piece, slot],
            send_sem=scatter_send.at[piece, peer],
            recv_sem=scatter_recv.at[piece, slot],
            device_id={"tp": peer},
            device_id_type=MESH,
        )

    def relay_to_mate(piece, block):
        return pltpu.make_async_remote_copy(
            src_ref=outgoing.at[piece, block],
            dst_ref=relay.at[piece, block],
            send_sem=scatter_send.at[piece, block],
            recv_sem=relay_recv.at[piece, block],
            device_id={"tp": mate},
            device_id_type=MESH,
        )

    def combine(piece):
        def add(peer):
            @pl.when(is_relay_for(peer))
            def _():
                relay_to_mate(piece, peer).wait_recv()
                outgoing[piece, peer] = (
                    outgoing[piece, peer].astype(F32) + relay[piece, peer].astype(F32)
                ).astype(BF16)
                scatter_to(piece, z, peer).start()

        each_peer(add)

    for piece in range(PIECES):
        share = jnp.zeros((total, cut), F32)
        for part in range(3):
            share += lax.dot_general(
                dproj[part],
                weight[part, piece * cut : (piece + 1) * cut, :],
                (((1,), (1,)), ((), ())),
                preferred_element_type=F32,
            )
        for block in range(n):
            outgoing[piece, block] = share[block * rows : (block + 1) * rows].astype(BF16)

        def hand_over(peer):
            @pl.when(jnp.logical_not(is_relay_for(peer)) & (peer != mate))
            def _():
                relay_to_mate(piece, peer).start()

        each_peer(hand_over)
        scatter_to(piece, z, mate).start()
        if piece > 0:
            combine(piece - 1)
    combine(PIECES - 1)

    @pl.when(has_before)
    def _():
        grad_copy.wait_send()
        first_rows.wait_send()

    @pl.when(has_after)
    def _():
        last_rows.wait_send()

    for piece in range(PIECES):

        def drain(peer):
            @pl.when((peer == mate) | faces(peer))
            def _():
                send_own(piece, peer).wait_send()

            @pl.when(is_relay_for(peer))
            def _():
                forward_to_mate(piece, peer).wait_send()

            scatter_to(piece, z, peer).wait_send()

        each_peer(drain)

    def result_copy(piece):
        return pltpu.make_async_copy(
            grad_tokens.at[piece],
            grad_tokens_hbm.at[:, pl.ds(piece * cut, cut)],
            token_sem.at[piece],
        )

    for piece in range(PIECES):
        scatter_to(piece, mate, mate).wait_recv()
        summed[...] = outgoing[piece, z].astype(F32) + incoming[piece, mate].astype(F32)

        def gain(peer):
            @pl.when(faces(peer) & (peer != mate))
            def _():
                scatter_to(piece, peer, peer).wait_recv()
                summed[...] += incoming[piece, peer].astype(F32)

        each_peer(gain)
        grad_tokens[piece] = summed[...].astype(BF16)
        result_copy(piece).start()

    for piece in range(PIECES):
        result_copy(piece).wait()

    gated_copy.wait()


def local(n, n_ctx, tokens, proj_weight, feat_taps, inner_taps, grad_out):
    rows, width = tokens.shape
    total, channels = grad_out.shape
    cut = width // PIECES
    weight = jnp.transpose(proj_weight, (1, 0, 2))
    anywhere = pl.BlockSpec(memory_space=pl.ANY)
    dma = pltpu.SemaphoreType.DMA
    long = total + 2 * HALO
    return pl.pallas_call(
        functools.partial(kernel, n, n_ctx),
        out_shape=(
            jax.ShapeDtypeStruct((total, channels), BF16),
            jax.ShapeDtypeStruct((rows, width), BF16),
        ),
        in_specs=[anywhere] * 5,
        out_specs=(anywhere, anywhere),
        scratch_shapes=[
            pltpu.VMEM((total, channels), BF16),
            pltpu.VMEM((PIECES, rows, cut), BF16),
            pltpu.VMEM(feat_taps.shape, F32),
            pltpu.VMEM(inner_taps.shape, F32),
            pltpu.VMEM((total, channels), BF16),
            pltpu.VMEM((3, width, channels), BF16),
            pltpu.VMEM((PIECES, n, rows, cut), BF16),
            pltpu.VMEM((total, 2 * cut), F32),
            pltpu.VMEM((3, long, channels), F32),
            pltpu.VMEM((total + HALO, channels), F32),
            pltpu.VMEM((long, channels), F32),
            pltpu.VMEM((long, channels), F32),
            pltpu.VMEM((3, long, channels), F32),
            pltpu.VMEM((3, total, channels), BF16),
            pltpu.VMEM((2, 3, HALO, channels), F32),
            pltpu.VMEM((2, 3, HALO, channels), F32),
            pltpu.VMEM((HALO, channels), F32),
            pltpu.VMEM((HALO, channels), F32),
            pltpu.VMEM((PIECES, n, rows, cut), BF16),
            pltpu.VMEM((PIECES, n, rows, cut), BF16),
            pltpu.VMEM((PIECES, n, rows, cut), BF16),
            pltpu.VMEM((rows, cut), F32),
            dma((PIECES, 3)),
            dma((PIECES, n)),
            dma((PIECES, n)),
            dma((PIECES, n)),
            dma((PIECES, n)),
            dma((PIECES, n)),
            dma((PIECES, n)),
            dma((3,)),
            dma((3,)),
            dma((PIECES,)),
            dma((4,)),
        ],
        compiler_params=pltpu.CompilerParams(
            collective_id=0, has_side_effects=True, vmem_limit_bytes=56 * 1024 * 1024
        ),
        cost_estimate=pl.CostEstimate(
            flops=4 * total * width * 3 * channels,
            bytes_accessed=6 * width * channels,
            transcendentals=0,
        ),
    )(tokens, weight, feat_taps, inner_taps, grad_out)


def solution(mesh):
    in_specs = (
        P(("ctx", "tp"), None),
        P(None, None, "tp"),
        P(None, None, "tp"),
        P(None, "tp"),
        P("ctx", "tp"),
    )
    out_specs = (P("ctx", "tp"), P(("ctx", "tp"), None))
    body = functools.partial(local, mesh.shape["tp"], mesh.shape["ctx"])
    return jax.shard_map(
        body, mesh=mesh, in_specs=in_specs, out_specs=out_specs, check_vma=False
    )
```

```python
import functools

import jax
import jax.numpy as jnp
from jax import lax
from jax.experimental import pallas as pl
from jax.experimental.pallas import tpu as pltpu
from jax.sharding import PartitionSpec as P

MESH = pl.DeviceIdType.MESH
F32 = jnp.float32
BF16 = jnp.bfloat16
PIECES = 8
GROUPS = ((0, 1), (2, 3), (4, 5), (6,), (7,))
RELAYED_GATHER = 4
RELAYED_SCATTER = 6
HALO = 8


def kernel(
    n,
    n_ctx,
    tokens,
    weight_hbm,
    feat_hbm,
    inner_hbm,
    grad_hbm,
    gated_hbm,
    grad_tokens_hbm,
    gated,
    grad_tokens,
    feat_taps,
    inner_taps,
    grad_out,
    weight,
    blocks,
    stack,
    ext,
    grads,
    mix,
    dinner,
    dfeat,
    dproj,
    edge,
    halo,
    grad_edge,
    grad_halo,
    outgoing,
    incoming,
    relay,
    summed,
    weight_sem,
    gather_recv,
    gather_send,
    forward_send,
    relay_recv,
    scatter_recv,
    scatter_send,
    halo_send,
    halo_recv,
    token_sem,
    small_sem,
):
    z = lax.axis_index("tp")
    ctx = lax.axis_index("ctx")
    rows, width = tokens.shape
    total, channels = gated.shape
    edge_rows = 2 * HALO
    cut = width // PIECES

    def weight_copy(piece, part):
        span = pl.ds(piece * cut, cut)
        return pltpu.make_async_copy(
            weight_hbm.at[part, span, :], weight.at[part, span, :], weight_sem.at[piece, part]
        )

    own = [
        pltpu.make_async_copy(
            tokens.at[:, pl.ds(piece * cut, cut)], blocks.at[piece, z], token_sem.at[piece]
        )
        for piece in range(PIECES)
    ]
    small = [
        pltpu.make_async_copy(source, target, small_sem.at[index])
        for index, (source, target) in enumerate(
            ((grad_hbm, grad_out), (feat_hbm, feat_taps), (inner_hbm, inner_taps))
        )
    ]
    has_before, has_after = ctx > 0, ctx < n_ctx - 1
    barrier = pltpu.get_barrier_semaphore()

    def each_peer(act):
        def visit(index, carry):
            far = n - 1 - index

            @pl.when(z + far < n)
            def _():
                act(z + far)

            @pl.when(z >= far)
            def _():
                act(z - far)

            return carry

        if n <= 8:
            for index in range(n - 1):
                visit(index, 0)
        else:
            lax.fori_loop(0, n - 1, visit, 0)

    mate = z + 1 - 2 * lax.rem(z, 2)
    even = lax.rem(z, 2) == 0

    def faces(peer):
        parity = lax.rem(peer, 2)
        return ((peer > z) & (parity == 0)) | ((peer < z) & (parity == 1))

    def is_relay_for(peer):
        return (even & (peer < z)) | (jnp.logical_not(even) & (peer > z))

    def greet(here, axis, index):
        @pl.when(here)
        def _():
            pl.semaphore_signal(barrier, inc=1, device_id={axis: index}, device_id_type=MESH)

    def greet_peer(peer):
        pl.semaphore_signal(barrier, inc=1, device_id={"tp": peer}, device_id_type=MESH)

    each_peer(greet_peer)
    greet(has_before, "ctx", ctx - 1)
    greet(has_after, "ctx", ctx + 1)

    for copy in own + small:
        copy.start()
    for part in range(3):
        weight_copy(0, part).start()

    peers = n - 1 + has_before.astype(jnp.int32) + has_after.astype(jnp.int32)
    pl.semaphore_wait(barrier, peers)

    def send_own(piece, peer):
        return pltpu.make_async_remote_copy(
            src_ref=tokens.at[:, pl.ds(piece * cut, cut)],
            dst_ref=blocks.at[piece, z],
            send_sem=gather_send.at[piece, peer],
            recv_sem=gather_recv.at[piece, z],
            device_id={"tp": peer},
            device_id_type=MESH,
        )

    def gather_to(piece, block, peer):
        return pltpu.make_async_remote_copy(
            src_ref=blocks.at[piece, block],
            dst_ref=blocks.at[piece, block],
            send_sem=gather_send.at[piece, peer],
            recv_sem=gather_recv.at[piece, block],
            device_id={"tp": peer},
            device_id_type=MESH,
        )

    def forward_to_mate(piece, block):
        return pltpu.make_async_remote_copy(
            src_ref=blocks.at[piece, block],
            dst_ref=blocks.at[piece, block],
            send_sem=forward_send.at[piece, block],
            recv_sem=gather_recv.at[piece, block],
            device_id={"tp": mate},
            device_id_type=MESH,
        )

    def spread(piece):
        def send(peer):
            @pl.when((peer == mate) | faces(peer))
            def _():
                send_own(piece, peer).start()

        if piece < RELAYED_GATHER:
            each_peer(send)
        else:
            each_peer(lambda peer: send_own(piece, peer).start())

    for piece in range(PIECES):
        spread(piece)

    for piece in range(1, PIECES):
        for part in range(3):
            weight_copy(piece, part).start()

    for copy in own + small:
        copy.wait()
    grads[0:total, :] = grad_out[...].astype(F32)
    grad_edge[...] = grads[0:HALO, :]

    grad_copy = pltpu.make_async_remote_copy(
        src_ref=grad_edge,
        dst_ref=grad_halo,
        send_sem=halo_send.at[0],
        recv_sem=halo_recv.at[0],
        device_id={"ctx": ctx - 1},
        device_id_type=MESH,
    )

    @pl.when(has_before)
    def _():
        grad_copy.start()

    def collect(piece):
        def take(peer):
            @pl.when(is_relay_for(peer))
            def _():
                gather_to(piece, peer, peer).wait_recv()
                forward_to_mate(piece, peer).start()

        def take_rest(peer):
            @pl.when(jnp.logical_not(is_relay_for(peer)))
            def _():
                gather_to(piece, peer, peer).wait_recv()

        if piece < RELAYED_GATHER:
            each_peer(take)
            each_peer(take_rest)
        else:
            each_peer(lambda peer: gather_to(piece, peer, peer).wait_recv())

    for group in GROUPS:
        for place, piece in enumerate(group):
            collect(piece)
            for block in range(n):
                stack[block * rows : (block + 1) * rows, place * cut : (place + 1) * cut] = (
                    blocks[piece, block].astype(F32)
                )
            for part in range(3):
                weight_copy(piece, part).wait()
        depth = len(group) * cut
        left_side = stack[:, 0:depth].astype(BF16)
        first = group[0] * cut
        for part in range(3):
            product = jnp.dot(
                left_side,
                weight[part, first : first + depth, :],
                preferred_element_type=F32,
            )
            if group[0] == 0:
                ext[part, HALO : HALO + total, :] = product
            else:
                ext[part, HALO : HALO + total, :] += product

    edge[0] = ext[:, HALO : 2 * HALO, :]
    edge[1] = ext[:, total : total + HALO, :]

    def edge_copy(side, target):
        return pltpu.make_async_remote_copy(
            src_ref=edge.at[side],
            dst_ref=halo.at[side],
            send_sem=halo_send.at[1 + side],
            recv_sem=halo_recv.at[1 + side],
            device_id={"ctx": target},
            device_id_type=MESH,
        )

    first_rows = edge_copy(0, ctx - 1)
    last_rows = edge_copy(1, ctx + 1)

    @pl.when(has_before)
    def _():
        first_rows.start()

    @pl.when(has_after)
    def _():
        last_rows.start()

    for scratch in (mix, dinner, dfeat):
        scratch[...] = jnp.zeros(scratch.shape, F32)

    def convolve(top, count, at):
        long = count + HALO

        def conv(part, start):
            terms = feat_taps[part, 0:1, at] * ext[part, start : start + long, at]
            for tap in range(1, 3):
                terms += (
                    feat_taps[part, tap : tap + 1, at]
                    * ext[part, start - tap : start - tap + long, at]
                )
            return terms

        cotangent = grads[top : top + long, at]
        query = conv(0, top + HALO)
        dinner[0:long, at] = cotangent * query
        key = conv(1, top + 2)
        value = conv(2, top + 2)
        mix[0:long, at] = key * value
        dfeat[1, 0:long, at] = value
        dfeat[2, 0:long, at] = key
        inner = inner_taps[0:1, at] * mix[6 : 6 + long, at]
        for tap in range(1, 7):
            inner += inner_taps[tap : tap + 1, at] * mix[6 - tap : 6 - tap + long, at]
        gated[top : top + count, at] = (query * inner)[0:count].astype(BF16)
        dfeat[0, 0:long, at] = cotangent * inner
        dmix = inner_taps[0:1, at] * dinner[0:long, at]
        for tap in range(1, 7):
            dmix += inner_taps[tap : tap + 1, at] * dinner[tap : tap + long, at]
        dkey = dmix * dfeat[1, 6 : 6 + long, at]
        dvalue = dmix * dfeat[2, 6 : 6 + long, at]
        dfeat[1, 0:long, at] = dkey
        dfeat[2, 0:long, at] = dvalue
        for part in range(3):
            series = feat_taps[part, 0:1, at] * dfeat[part, 0:count, at]
            for tap in range(1, 3):
                series += feat_taps[part, tap : tap + 1, at] * dfeat[part, tap : tap + count, at]
            dproj[part, top : top + count, at] = series.astype(BF16)

    def each_lanes(act):
        def visit(index, carry):
            act(pl.ds(pl.multiple_of(index * 128, 128), 128))
            return carry

        lax.fori_loop(0, channels // 128, visit, 0)

    each_lanes(lambda at: convolve(edge_rows, total - 2 * edge_rows, at))

    @pl.when(has_after)
    def _():
        grad_copy.wait_recv()
        grads[total : total + HALO, :] = grad_halo[...]
        first_rows.wait_recv()
        ext[:, HALO + total :, :] = halo[0]

    @pl.when(ctx == n_ctx - 1)
    def _():
        grads[total : total + HALO, :] = jnp.zeros((HALO, channels), F32)
        ext[:, HALO + total :, :] = jnp.zeros((3, HALO, channels), F32)

    @pl.when(has_before)
    def _():
        last_rows.wait_recv()
        ext[:, 0:HALO, :] = halo[1]

    @pl.when(ctx == 0)
    def _():
        ext[:, 0:HALO, :] = jnp.zeros((3, HALO, channels), F32)

    def edges(at):
        convolve(0, edge_rows, at)
        convolve(total - edge_rows, edge_rows, at)

    each_lanes(edges)
    gated_copy = pltpu.make_async_copy(gated, gated_hbm, small_sem.at[3])
    gated_copy.start()

    def scatter_to(piece, slot, peer):
        return pltpu.make_async_remote_copy(
            src_ref=outgoing.at[piece, peer],
            dst_ref=incoming.at[piece, slot],
            send_sem=scatter_send.at[piece, peer],
            recv_sem=scatter_recv.at[piece, slot],
            device_id={"tp": peer},
            device_id_type=MESH,
        )

    def relay_to_mate(piece, block):
        return pltpu.make_async_remote_copy(
            src_ref=outgoing.at[piece, block],
            dst_ref=relay.at[piece, block],
            send_sem=scatter_send.at[piece, block],
            recv_sem=relay_recv.at[piece, block],
            device_id={"tp": mate},
            device_id_type=MESH,
        )

    def combine(piece):
        def add(peer):
            @pl.when(is_relay_for(peer))
            def _():
                relay_to_mate(piece, peer).wait_recv()
                outgoing[piece, peer] = (
                    outgoing[piece, peer].astype(F32) + relay[piece, peer].astype(F32)
                ).astype(BF16)
                scatter_to(piece, z, peer).start()

        each_peer(add)

    for piece in range(PIECES):
        share = jnp.zeros((total, cut), F32)
        for part in range(3):
            share += lax.dot_general(
                dproj[part],
                weight[part, piece * cut : (piece + 1) * cut, :],
                (((1,), (1,)), ((), ())),
                preferred_element_type=F32,
            )
        for block in range(n):
            outgoing[piece, block] = share[block * rows : (block + 1) * rows].astype(BF16)

        def hand_over(peer):
            @pl.when(jnp.logical_not(is_relay_for(peer)) & (peer != mate))
            def _():
                relay_to_mate(piece, peer).start()

        if piece < RELAYED_SCATTER:
            each_peer(hand_over)
            scatter_to(piece, z, mate).start()
        else:
            each_peer(lambda peer: scatter_to(piece, z, peer).start())
        if 0 < piece <= RELAYED_SCATTER:
            combine(piece - 1)

    @pl.when(has_before)
    def _():
        grad_copy.wait_send()
        first_rows.wait_send()

    @pl.when(has_after)
    def _():
        last_rows.wait_send()

    for piece in range(PIECES):

        def drain(peer):
            if piece < RELAYED_GATHER:

                @pl.when((peer == mate) | faces(peer))
                def _():
                    send_own(piece, peer).wait_send()

                @pl.when(is_relay_for(peer))
                def _():
                    forward_to_mate(piece, peer).wait_send()

            else:
                send_own(piece, peer).wait_send()
            scatter_to(piece, z, peer).wait_send()

        each_peer(drain)

    def result_copy(piece):
        return pltpu.make_async_copy(
            grad_tokens.at[piece],
            grad_tokens_hbm.at[:, pl.ds(piece * cut, cut)],
            token_sem.at[piece],
        )

    for piece in range(PIECES):
        scatter_to(piece, mate, mate).wait_recv()
        summed[...] = outgoing[piece, z].astype(F32) + incoming[piece, mate].astype(F32)

        def gain(peer):
            sends = faces(peer) if piece < RELAYED_SCATTER else peer != mate

            @pl.when(sends)
            def _():
                scatter_to(piece, peer, peer).wait_recv()
                summed[...] += incoming[piece, peer].astype(F32)

        each_peer(gain)
        grad_tokens[piece] = summed[...].astype(BF16)
        result_copy(piece).start()

    for piece in range(PIECES):
        result_copy(piece).wait()

    gated_copy.wait()


def local(n, n_ctx, tokens, proj_weight, feat_taps, inner_taps, grad_out):
    rows, width = tokens.shape
    total, channels = grad_out.shape
    cut = width // PIECES
    weight = jnp.transpose(proj_weight, (1, 0, 2))
    anywhere = pl.BlockSpec(memory_space=pl.ANY)
    dma = pltpu.SemaphoreType.DMA
    long = total + 2 * HALO
    return pl.pallas_call(
        functools.partial(kernel, n, n_ctx),
        out_shape=(
            jax.ShapeDtypeStruct((total, channels), BF16),
            jax.ShapeDtypeStruct((rows, width), BF16),
        ),
        in_specs=[anywhere] * 5,
        out_specs=(anywhere, anywhere),
        scratch_shapes=[
            pltpu.VMEM((total, channels), BF16),
            pltpu.VMEM((PIECES, rows, cut), BF16),
            pltpu.VMEM(feat_taps.shape, F32),
            pltpu.VMEM(inner_taps.shape, F32),
            pltpu.VMEM((total, channels), BF16),
            pltpu.VMEM((3, width, channels), BF16),
            pltpu.VMEM((PIECES, n, rows, cut), BF16),
            pltpu.VMEM((total, 2 * cut), F32),
            pltpu.VMEM((3, long, channels), F32),
            pltpu.VMEM((total + HALO, channels), F32),
            pltpu.VMEM((long, channels), F32),
            pltpu.VMEM((long, channels), F32),
            pltpu.VMEM((3, long, channels), F32),
            pltpu.VMEM((3, total, channels), BF16),
            pltpu.VMEM((2, 3, HALO, channels), F32),
            pltpu.VMEM((2, 3, HALO, channels), F32),
            pltpu.VMEM((HALO, channels), F32),
            pltpu.VMEM((HALO, channels), F32),
            pltpu.VMEM((PIECES, n, rows, cut), BF16),
            pltpu.VMEM((PIECES, n, rows, cut), BF16),
            pltpu.VMEM((PIECES, n, rows, cut), BF16),
            pltpu.VMEM((rows, cut), F32),
            dma((PIECES, 3)),
            dma((PIECES, n)),
            dma((PIECES, n)),
            dma((PIECES, n)),
            dma((PIECES, n)),
            dma((PIECES, n)),
            dma((PIECES, n)),
            dma((3,)),
            dma((3,)),
            dma((PIECES,)),
            dma((4,)),
        ],
        compiler_params=pltpu.CompilerParams(
            collective_id=0, has_side_effects=True, vmem_limit_bytes=56 * 1024 * 1024
        ),
        cost_estimate=pl.CostEstimate(
            flops=4 * total * width * 3 * channels,
            bytes_accessed=6 * width * channels,
            transcendentals=0,
        ),
    )(tokens, weight, feat_taps, inner_taps, grad_out)


def solution(mesh):
    in_specs = (
        P(("ctx", "tp"), None),
        P(None, None, "tp"),
        P(None, None, "tp"),
        P(None, "tp"),
        P("ctx", "tp"),
    )
    out_specs = (P("ctx", "tp"), P(("ctx", "tp"), None))
    body = functools.partial(local, mesh.shape["tp"], mesh.shape["ctx"])
    return jax.shard_map(
        body, mesh=mesh, in_specs=in_specs, out_specs=out_specs, check_vma=False
    )
```

```python
import functools

import jax
import jax.numpy as jnp
from jax import lax
from jax.experimental import pallas as pl
from jax.experimental.pallas import tpu as pltpu
from jax.sharding import PartitionSpec as P

MESH = pl.DeviceIdType.MESH
F32 = jnp.float32
BF16 = jnp.bfloat16
PIECES = 8
GROUPS = ((0, 1), (2, 3), (4, 5), (6,), (7,))
HALO = 8


def kernel(
    n,
    n_ctx,
    tokens,
    weight_hbm,
    feat_hbm,
    inner_hbm,
    grad_hbm,
    gated_hbm,
    grad_tokens_hbm,
    gated,
    grad_tokens,
    feat_taps,
    inner_taps,
    grad_out,
    weight,
    blocks,
    stack,
    ext,
    grads,
    mix,
    dinner,
    dfeat,
    dproj,
    edge,
    halo,
    grad_edge,
    grad_halo,
    outgoing,
    incoming,
    relay,
    summed,
    weight_sem,
    gather_recv,
    gather_send,
    forward_send,
    relay_recv,
    scatter_recv,
    scatter_send,
    halo_send,
    halo_recv,
    token_sem,
    small_sem,
):
    z = lax.axis_index("tp")
    ctx = lax.axis_index("ctx")
    rows, width = tokens.shape
    total, channels = gated.shape
    edge_rows = 2 * HALO
    cut = width // PIECES

    def weight_copy(piece, part):
        span = pl.ds(piece * cut, cut)
        return pltpu.make_async_copy(
            weight_hbm.at[part, span, :], weight.at[part, span, :], weight_sem.at[piece, part]
        )

    own = [
        pltpu.make_async_copy(
            tokens.at[:, pl.ds(piece * cut, cut)], blocks.at[piece, z], token_sem.at[piece]
        )
        for piece in range(PIECES)
    ]
    small = [
        pltpu.make_async_copy(source, target, small_sem.at[index])
        for index, (source, target) in enumerate(
            ((grad_hbm, grad_out), (feat_hbm, feat_taps), (inner_hbm, inner_taps))
        )
    ]
    has_before, has_after = ctx > 0, ctx < n_ctx - 1
    barrier = pltpu.get_barrier_semaphore()

    def each_peer(act):
        def visit(index, carry):
            far = n - 1 - index

            @pl.when(z + far < n)
            def _():
                act(z + far)

            @pl.when(z >= far)
            def _():
                act(z - far)

            return carry

        if n <= 8:
            for index in range(n - 1):
                visit(index, 0)
        else:
            lax.fori_loop(0, n - 1, visit, 0)

    mate = z + 1 - 2 * lax.rem(z, 2)
    even = lax.rem(z, 2) == 0

    def faces(peer):
        parity = lax.rem(peer, 2)
        return ((peer > z) & (parity == 0)) | ((peer < z) & (parity == 1))

    def is_relay_for(peer):
        return (even & (peer < z)) | (jnp.logical_not(even) & (peer > z))

    def greet(here, axis, index):
        @pl.when(here)
        def _():
            pl.semaphore_signal(barrier, inc=1, device_id={axis: index}, device_id_type=MESH)

    def greet_peer(peer):
        pl.semaphore_signal(barrier, inc=1, device_id={"tp": peer}, device_id_type=MESH)

    each_peer(greet_peer)
    greet(has_before, "ctx", ctx - 1)
    greet(has_after, "ctx", ctx + 1)

    for copy in own + small:
        copy.start()
    for part in range(3):
        weight_copy(0, part).start()

    peers = n - 1 + has_before.astype(jnp.int32) + has_after.astype(jnp.int32)
    pl.semaphore_wait(barrier, peers)

    def send_own(piece, peer):
        return pltpu.make_async_remote_copy(
            src_ref=tokens.at[:, pl.ds(piece * cut, cut)],
            dst_ref=blocks.at[piece, z],
            send_sem=gather_send.at[piece, peer],
            recv_sem=gather_recv.at[piece, z],
            device_id={"tp": peer},
            device_id_type=MESH,
        )

    def gather_to(piece, block, peer):
        return pltpu.make_async_remote_copy(
            src_ref=blocks.at[piece, block],
            dst_ref=blocks.at[piece, block],
            send_sem=gather_send.at[piece, peer],
            recv_sem=gather_recv.at[piece, block],
            device_id={"tp": peer},
            device_id_type=MESH,
        )

    def forward_to_mate(piece, block):
        return pltpu.make_async_remote_copy(
            src_ref=blocks.at[piece, block],
            dst_ref=blocks.at[piece, block],
            send_sem=forward_send.at[piece, block],
            recv_sem=gather_recv.at[piece, block],
            device_id={"tp": mate},
            device_id_type=MESH,
        )

    def spread(piece):
        def send(peer):
            @pl.when((peer == mate) | faces(peer))
            def _():
                send_own(piece, peer).start()

        each_peer(send)

    for piece in range(PIECES):
        spread(piece)

    for piece in range(1, PIECES):
        for part in range(3):
            weight_copy(piece, part).start()

    for copy in own + small:
        copy.wait()
    grads[0:total, :] = grad_out[...].astype(F32)
    grad_edge[...] = grads[0:HALO, :]

    grad_copy = pltpu.make_async_remote_copy(
        src_ref=grad_edge,
        dst_ref=grad_halo,
        send_sem=halo_send.at[0],
        recv_sem=halo_recv.at[0],
        device_id={"ctx": ctx - 1},
        device_id_type=MESH,
    )

    @pl.when(has_before)
    def _():
        grad_copy.start()

    def collect(piece):
        def take(peer):
            @pl.when(is_relay_for(peer))
            def _():
                gather_to(piece, peer, peer).wait_recv()
                forward_to_mate(piece, peer).start()

        def take_rest(peer):
            @pl.when(jnp.logical_not(is_relay_for(peer)))
            def _():
                gather_to(piece, peer, peer).wait_recv()

        each_peer(take)
        each_peer(take_rest)

    for group in GROUPS:
        for place, piece in enumerate(group):
            collect(piece)
            for block in range(n):
                stack[block * rows : (block + 1) * rows, place * cut : (place + 1) * cut] = (
                    blocks[piece, block].astype(F32)
                )
            for part in range(3):
                weight_copy(piece, part).wait()
        depth = len(group) * cut
        left_side = stack[:, 0:depth].astype(BF16)
        first = group[0] * cut
        for part in range(3):
            product = jnp.dot(
                left_side,
                weight[part, first : first + depth, :],
                preferred_element_type=F32,
            )
            if group[0] == 0:
                ext[part, HALO : HALO + total, :] = product
            else:
                ext[part, HALO : HALO + total, :] += product

    edge[0] = ext[:, HALO : 2 * HALO, :]
    edge[1] = ext[:, total : total + HALO, :]

    def edge_copy(side, target):
        return pltpu.make_async_remote_copy(
            src_ref=edge.at[side],
            dst_ref=halo.at[side],
            send_sem=halo_send.at[1 + side],
            recv_sem=halo_recv.at[1 + side],
            device_id={"ctx": target},
            device_id_type=MESH,
        )

    first_rows = edge_copy(0, ctx - 1)
    last_rows = edge_copy(1, ctx + 1)

    @pl.when(has_before)
    def _():
        first_rows.start()

    @pl.when(has_after)
    def _():
        last_rows.start()

    for scratch in (mix, dinner, dfeat):
        scratch[...] = jnp.zeros(scratch.shape, F32)

    def convolve(top, count, at, base=0):
        long = count + HALO

        def conv(part, start):
            terms = feat_taps[part, 0:1, at] * ext[part, start : start + long, at]
            for tap in range(1, 3):
                terms += (
                    feat_taps[part, tap : tap + 1, at]
                    * ext[part, start - tap : start - tap + long, at]
                )
            return terms

        cotangent = grads[top : top + long, at]
        query = conv(0, top + HALO)
        dinner[base : base + long, at] = cotangent * query
        key = conv(1, top + 2)
        value = conv(2, top + 2)
        mix[base : base + long, at] = key * value
        dfeat[1, base : base + long, at] = value
        dfeat[2, base : base + long, at] = key
        inner = inner_taps[0:1, at] * mix[base + 6 : base + 6 + long, at]
        for tap in range(1, 7):
            inner += inner_taps[tap : tap + 1, at] * mix[base + 6 - tap : base + 6 - tap + long, at]
        gated[top : top + count, at] = (query * inner)[0:count].astype(BF16)
        dfeat[0, base : base + long, at] = cotangent * inner
        dmix = inner_taps[0:1, at] * dinner[base : base + long, at]
        for tap in range(1, 7):
            dmix += inner_taps[tap : tap + 1, at] * dinner[base + tap : base + tap + long, at]
        dkey = dmix * dfeat[1, base + 6 : base + 6 + long, at]
        dvalue = dmix * dfeat[2, base + 6 : base + 6 + long, at]
        dfeat[1, base : base + long, at] = dkey
        dfeat[2, base : base + long, at] = dvalue
        for part in range(3):
            series = feat_taps[part, 0:1, at] * dfeat[part, base : base + count, at]
            for tap in range(1, 3):
                series += feat_taps[part, tap : tap + 1, at] * dfeat[part, base + tap : base + tap + count, at]
            dproj[part, top : top + count, at] = series.astype(BF16)

    def each_lanes(act):
        def visit(index, carry):
            act(pl.ds(pl.multiple_of(index * 128, 128), 128))
            return carry

        lax.fori_loop(0, channels // 128, visit, 0)

    each_lanes(lambda at: convolve(edge_rows, total - 2 * edge_rows, at))

    @pl.when(has_after)
    def _():
        grad_copy.wait_recv()
        grads[total : total + HALO, :] = grad_halo[...]
        first_rows.wait_recv()
        ext[:, HALO + total :, :] = halo[0]

    @pl.when(ctx == n_ctx - 1)
    def _():
        grads[total : total + HALO, :] = jnp.zeros((HALO, channels), F32)
        ext[:, HALO + total :, :] = jnp.zeros((3, HALO, channels), F32)

    @pl.when(has_before)
    def _():
        last_rows.wait_recv()
        ext[:, 0:HALO, :] = halo[1]

    @pl.when(ctx == 0)
    def _():
        ext[:, 0:HALO, :] = jnp.zeros((3, HALO, channels), F32)

    half = channels // 2 if channels % 256 == 0 else channels
    for start in range(0, channels, half):
        at = pl.ds(start, half)
        convolve(0, edge_rows, at)
        convolve(total - edge_rows, edge_rows, at, 4 * edge_rows)
    gated_copy = pltpu.make_async_copy(gated, gated_hbm, small_sem.at[3])
    gated_copy.start()

    def scatter_to(piece, slot, peer):
        return pltpu.make_async_remote_copy(
            src_ref=outgoing.at[piece, peer],
            dst_ref=incoming.at[piece, slot],
            send_sem=scatter_send.at[piece, peer],
            recv_sem=scatter_recv.at[piece, slot],
            device_id={"tp": peer},
            device_id_type=MESH,
        )

    def relay_to_mate(piece, block):
        return pltpu.make_async_remote_copy(
            src_ref=outgoing.at[piece, block],
            dst_ref=relay.at[piece, block],
            send_sem=scatter_send.at[piece, block],
            recv_sem=relay_recv.at[piece, block],
            device_id={"tp": mate},
            device_id_type=MESH,
        )

    def combine(piece):
        def add(peer):
            @pl.when(is_relay_for(peer))
            def _():
                relay_to_mate(piece, peer).wait_recv()
                outgoing[piece, peer] = (
                    outgoing[piece, peer].astype(F32) + relay[piece, peer].astype(F32)
                ).astype(BF16)
                scatter_to(piece, z, peer).start()

        each_peer(add)

    for piece in range(PIECES):
        share = jnp.zeros((total, cut), F32)
        for part in range(3):
            share += lax.dot_general(
                dproj[part],
                weight[part, piece * cut : (piece + 1) * cut, :],
                (((1,), (1,)), ((), ())),
                preferred_element_type=F32,
            )
        for block in range(n):
            outgoing[piece, block] = share[block * rows : (block + 1) * rows].astype(BF16)

        def hand_over(peer):
            @pl.when(jnp.logical_not(is_relay_for(peer)) & (peer != mate))
            def _():
                relay_to_mate(piece, peer).start()

        each_peer(hand_over)
        scatter_to(piece, z, mate).start()
        if piece > 0:
            combine(piece - 1)
    combine(PIECES - 1)

    @pl.when(has_before)
    def _():
        grad_copy.wait_send()
        first_rows.wait_send()

    @pl.when(has_after)
    def _():
        last_rows.wait_send()

    for piece in range(PIECES):

        def drain(peer):
            @pl.when((peer == mate) | faces(peer))
            def _():
                send_own(piece, peer).wait_send()

            @pl.when(is_relay_for(peer))
            def _():
                forward_to_mate(piece, peer).wait_send()

            scatter_to(piece, z, peer).wait_send()

        each_peer(drain)

    def result_copy(piece):
        return pltpu.make_async_copy(
            grad_tokens.at[piece],
            grad_tokens_hbm.at[:, pl.ds(piece * cut, cut)],
            token_sem.at[piece],
        )

    for piece in range(PIECES):
        scatter_to(piece, mate, mate).wait_recv()
        summed[...] = outgoing[piece, z].astype(F32) + incoming[piece, mate].astype(F32)

        def gain(peer):
            @pl.when(faces(peer) & (peer != mate))
            def _():
                scatter_to(piece, peer, peer).wait_recv()
                summed[...] += incoming[piece, peer].astype(F32)

        each_peer(gain)
        grad_tokens[piece] = summed[...].astype(BF16)
        result_copy(piece).start()

    for piece in range(PIECES):
        result_copy(piece).wait()

    gated_copy.wait()


def local(n, n_ctx, tokens, proj_weight, feat_taps, inner_taps, grad_out):
    rows, width = tokens.shape
    total, channels = grad_out.shape
    cut = width // PIECES
    weight = jnp.transpose(proj_weight, (1, 0, 2))
    anywhere = pl.BlockSpec(memory_space=pl.ANY)
    dma = pltpu.SemaphoreType.DMA
    long = total + 2 * HALO
    return pl.pallas_call(
        functools.partial(kernel, n, n_ctx),
        out_shape=(
            jax.ShapeDtypeStruct((total, channels), BF16),
            jax.ShapeDtypeStruct((rows, width), BF16),
        ),
        in_specs=[anywhere] * 5,
        out_specs=(anywhere, anywhere),
        scratch_shapes=[
            pltpu.VMEM((total, channels), BF16),
            pltpu.VMEM((PIECES, rows, cut), BF16),
            pltpu.VMEM(feat_taps.shape, F32),
            pltpu.VMEM(inner_taps.shape, F32),
            pltpu.VMEM((total, channels), BF16),
            pltpu.VMEM((3, width, channels), BF16),
            pltpu.VMEM((PIECES, n, rows, cut), BF16),
            pltpu.VMEM((total, 2 * cut), F32),
            pltpu.VMEM((3, long, channels), F32),
            pltpu.VMEM((total + HALO, channels), F32),
            pltpu.VMEM((long, channels), F32),
            pltpu.VMEM((long, channels), F32),
            pltpu.VMEM((3, long, channels), F32),
            pltpu.VMEM((3, total, channels), BF16),
            pltpu.VMEM((2, 3, HALO, channels), F32),
            pltpu.VMEM((2, 3, HALO, channels), F32),
            pltpu.VMEM((HALO, channels), F32),
            pltpu.VMEM((HALO, channels), F32),
            pltpu.VMEM((PIECES, n, rows, cut), BF16),
            pltpu.VMEM((PIECES, n, rows, cut), BF16),
            pltpu.VMEM((PIECES, n, rows, cut), BF16),
            pltpu.VMEM((rows, cut), F32),
            dma((PIECES, 3)),
            dma((PIECES, n)),
            dma((PIECES, n)),
            dma((PIECES, n)),
            dma((PIECES, n)),
            dma((PIECES, n)),
            dma((PIECES, n)),
            dma((3,)),
            dma((3,)),
            dma((PIECES,)),
            dma((4,)),
        ],
        compiler_params=pltpu.CompilerParams(
            collective_id=0, has_side_effects=True, vmem_limit_bytes=56 * 1024 * 1024
        ),
        cost_estimate=pl.CostEstimate(
            flops=4 * total * width * 3 * channels,
            bytes_accessed=6 * width * channels,
            transcendentals=0,
        ),
    )(tokens, weight, feat_taps, inner_taps, grad_out)


def solution(mesh):
    in_specs = (
        P(("ctx", "tp"), None),
        P(None, None, "tp"),
        P(None, None, "tp"),
        P(None, "tp"),
        P("ctx", "tp"),
    )
    out_specs = (P("ctx", "tp"), P(("ctx", "tp"), None))
    body = functools.partial(local, mesh.shape["tp"], mesh.shape["ctx"])
    return jax.shard_map(
        body, mesh=mesh, in_specs=in_specs, out_specs=out_specs, check_vma=False
    )
```

```python
import functools

import jax
import jax.numpy as jnp
from jax import lax
from jax.experimental import pallas as pl
from jax.experimental.pallas import tpu as pltpu
from jax.sharding import PartitionSpec as P

MESH = pl.DeviceIdType.MESH
F32 = jnp.float32
BF16 = jnp.bfloat16
PIECES = 8
GROUPS = ((0,), (1,), (2, 3), (4, 5), (6,), (7,))
HALO = 8


def kernel(
    n,
    n_ctx,
    tokens,
    weight_hbm,
    feat_hbm,
    inner_hbm,
    grad_hbm,
    gated_hbm,
    grad_tokens_hbm,
    gated,
    grad_tokens,
    feat_taps,
    inner_taps,
    grad_out,
    weight,
    blocks,
    stack,
    ext,
    grads,
    mix,
    dinner,
    dfeat,
    dproj,
    edge,
    halo,
    grad_edge,
    grad_halo,
    outgoing,
    incoming,
    relay,
    summed,
    weight_sem,
    gather_recv,
    gather_send,
    forward_send,
    relay_recv,
    scatter_recv,
    scatter_send,
    halo_send,
    halo_recv,
    token_sem,
    small_sem,
):
    z = lax.axis_index("tp")
    ctx = lax.axis_index("ctx")
    rows, width = tokens.shape
    total, channels = gated.shape
    edge_rows = 2 * HALO
    cut = width // PIECES

    def weight_copy(piece, part):
        span = pl.ds(piece * cut, cut)
        return pltpu.make_async_copy(
            weight_hbm.at[part, span, :], weight.at[part, span, :], weight_sem.at[piece, part]
        )

    own = [
        pltpu.make_async_copy(
            tokens.at[:, pl.ds(piece * cut, cut)], blocks.at[piece, z], token_sem.at[piece]
        )
        for piece in range(PIECES)
    ]
    small = [
        pltpu.make_async_copy(source, target, small_sem.at[index])
        for index, (source, target) in enumerate(
            ((grad_hbm, grad_out), (feat_hbm, feat_taps), (inner_hbm, inner_taps))
        )
    ]
    has_before, has_after = ctx > 0, ctx < n_ctx - 1
    barrier = pltpu.get_barrier_semaphore()

    def each_peer(act):
        def visit(index, carry):
            far = n - 1 - index

            @pl.when(z + far < n)
            def _():
                act(z + far)

            @pl.when(z >= far)
            def _():
                act(z - far)

            return carry

        if n <= 8:
            for index in range(n - 1):
                visit(index, 0)
        else:
            lax.fori_loop(0, n - 1, visit, 0)

    mate = z + 1 - 2 * lax.rem(z, 2)
    even = lax.rem(z, 2) == 0

    def faces(peer):
        parity = lax.rem(peer, 2)
        return ((peer > z) & (parity == 0)) | ((peer < z) & (parity == 1))

    def is_relay_for(peer):
        return (even & (peer < z)) | (jnp.logical_not(even) & (peer > z))

    def greet(here, axis, index):
        @pl.when(here)
        def _():
            pl.semaphore_signal(barrier, inc=1, device_id={axis: index}, device_id_type=MESH)

    def greet_peer(peer):
        pl.semaphore_signal(barrier, inc=1, device_id={"tp": peer}, device_id_type=MESH)

    each_peer(greet_peer)
    greet(has_before, "ctx", ctx - 1)
    greet(has_after, "ctx", ctx + 1)

    for copy in own + small:
        copy.start()
    for part in range(3):
        weight_copy(0, part).start()

    peers = n - 1 + has_before.astype(jnp.int32) + has_after.astype(jnp.int32)
    pl.semaphore_wait(barrier, peers)

    def send_own(piece, peer):
        return pltpu.make_async_remote_copy(
            src_ref=tokens.at[:, pl.ds(piece * cut, cut)],
            dst_ref=blocks.at[piece, z],
            send_sem=gather_send.at[piece, peer],
            recv_sem=gather_recv.at[piece, z],
            device_id={"tp": peer},
            device_id_type=MESH,
        )

    def gather_to(piece, block, peer):
        return pltpu.make_async_remote_copy(
            src_ref=blocks.at[piece, block],
            dst_ref=blocks.at[piece, block],
            send_sem=gather_send.at[piece, peer],
            recv_sem=gather_recv.at[piece, block],
            device_id={"tp": peer},
            device_id_type=MESH,
        )

    def forward_to_mate(piece, block):
        return pltpu.make_async_remote_copy(
            src_ref=blocks.at[piece, block],
            dst_ref=blocks.at[piece, block],
            send_sem=forward_send.at[piece, block],
            recv_sem=gather_recv.at[piece, block],
            device_id={"tp": mate},
            device_id_type=MESH,
        )

    def spread(piece):
        def send(peer):
            @pl.when((peer == mate) | faces(peer))
            def _():
                send_own(piece, peer).start()

        each_peer(send)

    for piece in range(PIECES):
        spread(piece)

    for piece in range(1, PIECES):
        for part in range(3):
            weight_copy(piece, part).start()

    for copy in own + small:
        copy.wait()
    grads[0:total, :] = grad_out[...].astype(F32)
    grad_edge[...] = grads[0:HALO, :]

    grad_copy = pltpu.make_async_remote_copy(
        src_ref=grad_edge,
        dst_ref=grad_halo,
        send_sem=halo_send.at[0],
        recv_sem=halo_recv.at[0],
        device_id={"ctx": ctx - 1},
        device_id_type=MESH,
    )

    @pl.when(has_before)
    def _():
        grad_copy.start()

    def collect(piece):
        def take(peer):
            @pl.when(is_relay_for(peer))
            def _():
                gather_to(piece, peer, peer).wait_recv()
                forward_to_mate(piece, peer).start()

        def take_rest(peer):
            @pl.when(jnp.logical_not(is_relay_for(peer)))
            def _():
                gather_to(piece, peer, peer).wait_recv()

        each_peer(take)
        each_peer(take_rest)

    for group in GROUPS:
        for place, piece in enumerate(group):
            collect(piece)
            for block in range(n):
                stack[block * rows : (block + 1) * rows, place * cut : (place + 1) * cut] = (
                    blocks[piece, block].astype(F32)
                )
            for part in range(3):
                weight_copy(piece, part).wait()
        depth = len(group) * cut
        left_side = stack[:, 0:depth].astype(BF16)
        first = group[0] * cut
        for part in range(3):
            product = jnp.dot(
                left_side,
                weight[part, first : first + depth, :],
                preferred_element_type=F32,
            )
            if group[0] == 0:
                ext[part, HALO : HALO + total, :] = product
            else:
                ext[part, HALO : HALO + total, :] += product

    edge[0] = ext[:, HALO : 2 * HALO, :]
    edge[1] = ext[:, total : total + HALO, :]

    def edge_copy(side, target):
        return pltpu.make_async_remote_copy(
            src_ref=edge.at[side],
            dst_ref=halo.at[side],
            send_sem=halo_send.at[1 + side],
            recv_sem=halo_recv.at[1 + side],
            device_id={"ctx": target},
            device_id_type=MESH,
        )

    first_rows = edge_copy(0, ctx - 1)
    last_rows = edge_copy(1, ctx + 1)

    @pl.when(has_before)
    def _():
        first_rows.start()

    @pl.when(has_after)
    def _():
        last_rows.start()

    for scratch in (mix, dinner, dfeat):
        scratch[...] = jnp.zeros(scratch.shape, F32)

    def convolve(top, count, at, base=0):
        long = count + HALO

        def conv(part, start):
            terms = feat_taps[part, 0:1, at] * ext[part, start : start + long, at]
            for tap in range(1, 3):
                terms += (
                    feat_taps[part, tap : tap + 1, at]
                    * ext[part, start - tap : start - tap + long, at]
                )
            return terms

        cotangent = grads[top : top + long, at]
        query = conv(0, top + HALO)
        dinner[base : base + long, at] = cotangent * query
        key = conv(1, top + 2)
        value = conv(2, top + 2)
        mix[base : base + long, at] = key * value
        dfeat[1, base : base + long, at] = value
        dfeat[2, base : base + long, at] = key
        inner = inner_taps[0:1, at] * mix[base + 6 : base + 6 + long, at]
        for tap in range(1, 7):
            inner += inner_taps[tap : tap + 1, at] * mix[base + 6 - tap : base + 6 - tap + long, at]
        gated[top : top + count, at] = (query * inner)[0:count].astype(BF16)
        dfeat[0, base : base + long, at] = cotangent * inner
        dmix = inner_taps[0:1, at] * dinner[base : base + long, at]
        for tap in range(1, 7):
            dmix += inner_taps[tap : tap + 1, at] * dinner[base + tap : base + tap + long, at]
        dkey = dmix * dfeat[1, base + 6 : base + 6 + long, at]
        dvalue = dmix * dfeat[2, base + 6 : base + 6 + long, at]
        dfeat[1, base : base + long, at] = dkey
        dfeat[2, base : base + long, at] = dvalue
        for part in range(3):
            series = feat_taps[part, 0:1, at] * dfeat[part, base : base + count, at]
            for tap in range(1, 3):
                series += feat_taps[part, tap : tap + 1, at] * dfeat[part, base + tap : base + tap + count, at]
            dproj[part, top : top + count, at] = series.astype(BF16)

    def each_lanes(act):
        def visit(index, carry):
            act(pl.ds(pl.multiple_of(index * 128, 128), 128))
            return carry

        lax.fori_loop(0, channels // 128, visit, 0)

    each_lanes(lambda at: convolve(edge_rows, total - 2 * edge_rows, at))

    @pl.when(has_after)
    def _():
        grad_copy.wait_recv()
        grads[total : total + HALO, :] = grad_halo[...]
        first_rows.wait_recv()
        ext[:, HALO + total :, :] = halo[0]

    @pl.when(ctx == n_ctx - 1)
    def _():
        grads[total : total + HALO, :] = jnp.zeros((HALO, channels), F32)
        ext[:, HALO + total :, :] = jnp.zeros((3, HALO, channels), F32)

    @pl.when(has_before)
    def _():
        last_rows.wait_recv()
        ext[:, 0:HALO, :] = halo[1]

    @pl.when(ctx == 0)
    def _():
        ext[:, 0:HALO, :] = jnp.zeros((3, HALO, channels), F32)

    half = channels // 2 if channels % 256 == 0 else channels
    for start in range(0, channels, half):
        at = pl.ds(start, half)
        convolve(0, edge_rows, at)
        convolve(total - edge_rows, edge_rows, at, 4 * edge_rows)
    gated_copy = pltpu.make_async_copy(gated, gated_hbm, small_sem.at[3])
    gated_copy.start()

    def scatter_to(piece, slot, peer):
        return pltpu.make_async_remote_copy(
            src_ref=outgoing.at[piece, peer],
            dst_ref=incoming.at[piece, slot],
            send_sem=scatter_send.at[piece, peer],
            recv_sem=scatter_recv.at[piece, slot],
            device_id={"tp": peer},
            device_id_type=MESH,
        )

    def relay_to_mate(piece, block):
        return pltpu.make_async_remote_copy(
            src_ref=outgoing.at[piece, block],
            dst_ref=relay.at[piece, block],
            send_sem=scatter_send.at[piece, block],
            recv_sem=relay_recv.at[piece, block],
            device_id={"tp": mate},
            device_id_type=MESH,
        )

    def combine(piece):
        def add(peer):
            @pl.when(is_relay_for(peer))
            def _():
                relay_to_mate(piece, peer).wait_recv()
                outgoing[piece, peer] = (
                    outgoing[piece, peer].astype(F32) + relay[piece, peer].astype(F32)
                ).astype(BF16)
                scatter_to(piece, z, peer).start()

        each_peer(add)

    for piece in range(PIECES):
        share = jnp.zeros((total, cut), F32)
        for part in range(3):
            share += lax.dot_general(
                dproj[part],
                weight[part, piece * cut : (piece + 1) * cut, :],
                (((1,), (1,)), ((), ())),
                preferred_element_type=F32,
            )
        for block in range(n):
            outgoing[piece, block] = share[block * rows : (block + 1) * rows].astype(BF16)

        def hand_over(peer):
            @pl.when(jnp.logical_not(is_relay_for(peer)) & (peer != mate))
            def _():
                relay_to_mate(piece, peer).start()

        each_peer(hand_over)
        scatter_to(piece, z, mate).start()
        if piece > 0:
            combine(piece - 1)
    combine(PIECES - 1)

    @pl.when(has_before)
    def _():
        grad_copy.wait_send()
        first_rows.wait_send()

    @pl.when(has_after)
    def _():
        last_rows.wait_send()

    for piece in range(PIECES):

        def drain(peer):
            @pl.when((peer == mate) | faces(peer))
            def _():
                send_own(piece, peer).wait_send()

            @pl.when(is_relay_for(peer))
            def _():
                forward_to_mate(piece, peer).wait_send()

            scatter_to(piece, z, peer).wait_send()

        each_peer(drain)

    def result_copy(piece):
        return pltpu.make_async_copy(
            grad_tokens.at[piece],
            grad_tokens_hbm.at[:, pl.ds(piece * cut, cut)],
            token_sem.at[piece],
        )

    for piece in range(PIECES):
        scatter_to(piece, mate, mate).wait_recv()
        summed[...] = outgoing[piece, z].astype(F32) + incoming[piece, mate].astype(F32)

        def gain(peer):
            @pl.when(faces(peer) & (peer != mate))
            def _():
                scatter_to(piece, peer, peer).wait_recv()
                summed[...] += incoming[piece, peer].astype(F32)

        each_peer(gain)
        grad_tokens[piece] = summed[...].astype(BF16)
        result_copy(piece).start()

    for piece in range(PIECES):
        result_copy(piece).wait()

    gated_copy.wait()


def local(n, n_ctx, tokens, proj_weight, feat_taps, inner_taps, grad_out):
    rows, width = tokens.shape
    total, channels = grad_out.shape
    cut = width // PIECES
    weight = jnp.transpose(proj_weight, (1, 0, 2))
    anywhere = pl.BlockSpec(memory_space=pl.ANY)
    dma = pltpu.SemaphoreType.DMA
    long = total + 2 * HALO
    return pl.pallas_call(
        functools.partial(kernel, n, n_ctx),
        out_shape=(
            jax.ShapeDtypeStruct((total, channels), BF16),
            jax.ShapeDtypeStruct((rows, width), BF16),
        ),
        in_specs=[anywhere] * 5,
        out_specs=(anywhere, anywhere),
        scratch_shapes=[
            pltpu.VMEM((total, channels), BF16),
            pltpu.VMEM((PIECES, rows, cut), BF16),
            pltpu.VMEM(feat_taps.shape, F32),
            pltpu.VMEM(inner_taps.shape, F32),
            pltpu.VMEM((total, channels), BF16),
            pltpu.VMEM((3, width, channels), BF16),
            pltpu.VMEM((PIECES, n, rows, cut), BF16),
            pltpu.VMEM((total, 2 * cut), F32),
            pltpu.VMEM((3, long, channels), F32),
            pltpu.VMEM((total + HALO, channels), F32),
            pltpu.VMEM((long, channels), F32),
            pltpu.VMEM((long, channels), F32),
            pltpu.VMEM((3, long, channels), F32),
            pltpu.VMEM((3, total, channels), BF16),
            pltpu.VMEM((2, 3, HALO, channels), F32),
            pltpu.VMEM((2, 3, HALO, channels), F32),
            pltpu.VMEM((HALO, channels), F32),
            pltpu.VMEM((HALO, channels), F32),
            pltpu.VMEM((PIECES, n, rows, cut), BF16),
            pltpu.VMEM((PIECES, n, rows, cut), BF16),
            pltpu.VMEM((PIECES, n, rows, cut), BF16),
            pltpu.VMEM((rows, cut), F32),
            dma((PIECES, 3)),
            dma((PIECES, n)),
            dma((PIECES, n)),
            dma((PIECES, n)),
            dma((PIECES, n)),
            dma((PIECES, n)),
            dma((PIECES, n)),
            dma((3,)),
            dma((3,)),
            dma((PIECES,)),
            dma((4,)),
        ],
        compiler_params=pltpu.CompilerParams(
            collective_id=0, has_side_effects=True, vmem_limit_bytes=56 * 1024 * 1024
        ),
        cost_estimate=pl.CostEstimate(
            flops=4 * total * width * 3 * channels,
            bytes_accessed=6 * width * channels,
            transcendentals=0,
        ),
    )(tokens, weight, feat_taps, inner_taps, grad_out)


def solution(mesh):
    in_specs = (
        P(("ctx", "tp"), None),
        P(None, None, "tp"),
        P(None, None, "tp"),
        P(None, "tp"),
        P("ctx", "tp"),
    )
    out_specs = (P("ctx", "tp"), P(("ctx", "tp"), None))
    body = functools.partial(local, mesh.shape["tp"], mesh.shape["ctx"])
    return jax.shard_map(
        body, mesh=mesh, in_specs=in_specs, out_specs=out_specs, check_vma=False
    )
```
